512 devices in a mesh: dp: 64 (over z_hi, x, y), seq: 8 (over z_lo, core).
Axes of the slice: x: 4, y: 4, z: 16 (z_hi: 4, z_lo: 4; z = z_hi * 4 + z_lo), core: 2. Of those that a mesh axis runs over, the one named last changes fastest.
Arguments:
- tokens: bfloat16 [32768, 2048], P(('dp', 'seq')), may hold values from -24 to 24
- proj_weight: bfloat16 [2048, 2048], P('dp', 'seq'), may hold values from -0.125 to 0.125
- cotangent: bfloat16 [32768, 2048], P('dp', 'seq'), may hold values from -0.75 to 0.75
- filters: float32 [7, 2048], P(None, 'seq'), may hold values from -6 to 6
Outputs:
- input_grad: bfloat16 [32768, 2048], P(('dp', 'seq'))
- weight_grad: bfloat16 [2048, 2048], P('dp', 'seq')
- filter_grad: float32 [7, 2048], P(None, 'seq')
The draws below stay inside these ranges and needn't reach their ends.
All inputs are finite; a program needn't handle non-finite values.
Results may differ from the reference program's by a relative error of at most 0.017.
Values may be sent and summed in bfloat16 or wider, within the bound.
No kernel may reach another device: no remote copies, remote signals or barrier semaphores. Data moves between devices by JAX's collectives and lax.ppermute only.
A program may use at most 64 MiB of HBM per device.

```python
import jax
import jax.numpy as jnp
from jax import lax

D = 2048
CH = 2048
TAPS = 7
TOKENS = 32768
N_SEQ = 8


def raised(values, own_key, source, target, blocks, factor):
    def block_of(axis_at):
        return (jnp.arange(values.shape[axis_at]) // (values.shape[axis_at] // blocks)).reshape((-1,) + (1,) * (values.ndim - 1 - axis_at))

    one_side = jax.random.permutation(own_key, blocks)[block_of(target)]
    other_side = (block_of(target) + blocks // 2) % blocks
    return jnp.where((block_of(source) == one_side) | (block_of(source) == other_side), factor * values, values)


def block_scale(key, shape, cuts, low, largest):
    loudness, own = 1.0, jax.random.fold_in(key, 6)
    for position, parts in cuts:
        steps = jnp.exp(jax.random.uniform(jax.random.fold_in(own, position), (parts,), jnp.float32, low / len(cuts), largest / len(cuts)))
        loudness = loudness * jnp.repeat(steps, shape[position] // parts).reshape([-1 if axis == position else 1 for axis in range(len(shape))])
    return loudness


def gaussian(own_key, shape, scale, most, shards=(), kind=jnp.bfloat16):
    factor_of = block_scale(own_key, shape, shards, -0.22, 0.18) if shards else 1.0
    values = jax.random.normal(own_key, shape, jnp.float32) * scale * factor_of
    return jnp.minimum(jnp.maximum(values, -most), most).astype(kind)


def heavy_noise(key, extent, spread, reach, pieces, heavy, held_as=jnp.bfloat16):
    result = spread * jax.random.normal(key, extent, jnp.float32)
    if pieces:
        result = result * block_scale(key, extent, pieces, -0.22, 0.18)
    return jnp.clip(raised(result, jax.random.fold_in(key, 3), *heavy), -reach, reach).astype(held_as)


def setup_inputs(seed: int = 0) -> dict:
    arg_keys = jax.random.split(jax.random.key(seed), 5)
    return {
        "tokens": heavy_noise(arg_keys[0], (TOKENS, D), 1.0, 24.0, ((0, 512),), (0, 1, 512, 6.0)),
        "proj_weight": gaussian(arg_keys[1], (D, CH), D ** -0.5, 0.125, ((0, 64), (1, 8))),
        "cotangent": gaussian(arg_keys[2], (TOKENS, CH), 0.05, 0.75, ((0, 64), (1, 8))),
        "filters": gaussian(arg_keys[3], (TAPS, CH), 0.5, 6.0, ((1, 8),), jnp.float32),
    }


def reference(tokens, proj_weight, cotangent, filters):
    featured = jnp.dot(tokens, proj_weight, preferred_element_type=jnp.float32).astype(jnp.bfloat16)
    feat_float = lax.optimization_barrier(featured).astype(jnp.float32)
    grad_float = cotangent.astype(jnp.float32)
    total_rows = grad_float.shape[0]
    extended = jnp.concatenate([grad_float, jnp.zeros((TAPS - 1, grad_float.shape[1]), jnp.float32)], 0)
    grad_feat = jnp.zeros_like(grad_float)
    filter_rows = []
    for tap_index in range(TAPS):
        window = extended[tap_index:tap_index + total_rows]
        grad_feat = grad_feat + filters[tap_index] * window
        filter_rows.append(jnp.sum(feat_float * window, axis=0))
    filter_grad = jnp.stack(filter_rows)
    grad_bf = grad_feat.astype(jnp.bfloat16)
    weight_grad = lax.dot_general(tokens, grad_bf, (((0,), (0,)), ((), ())), preferred_element_type=jnp.float32).astype(jnp.bfloat16)
    group_width = proj_weight.shape[1] // N_SEQ
    input_total = jnp.zeros((total_rows, tokens.shape[1]), jnp.float32)
    for shard in range(N_SEQ):
        lower = shard * group_width
        partial_grad = lax.dot_general(grad_bf[:, lower:lower + group_width], proj_weight[:, lower:lower + group_width], (((1,), (1,)), ((), ())), preferred_element_type=jnp.float32)
        rounded = lax.optimization_barrier(partial_grad.astype(jnp.bfloat16))
        input_total = input_total + rounded.astype(jnp.float32)
    return input_total.astype(jnp.bfloat16), weight_grad, filter_grad
```

```python
import jax
import jax.numpy as jnp
from jax import lax
from jax.sharding import Mesh, PartitionSpec as P

TAPS = 7
BF = jnp.bfloat16
F32 = jnp.float32
ZH, X, Y, ZL, C = "zh", "x", "y", "zl", "c"


def weight_columns(proj_weight):
    rows, cols = proj_weight.shape
    nz = lax.axis_size(ZH)
    nxy = lax.axis_size((X, Y))
    mine = lax.axis_index(ZH) == jnp.arange(nz)
    padded = jnp.where(mine[:, None, None], proj_weight[None], jnp.zeros((), BF))
    column = lax.psum(padded, ZH)
    repeated = jnp.broadcast_to(column[None], (nxy, nz, rows, cols))
    gathered = lax.all_to_all(repeated, (X, Y), split_axis=0, concat_axis=0, tiled=True)
    return gathered.transpose(1, 0, 2, 3).reshape(nz * nxy * rows, cols)


def body(tokens, proj_weight, cotangent, filters):
    nz = lax.axis_size(ZH)
    nxy = lax.axis_size((X, Y))
    nzl = lax.axis_size(ZL)
    ndp = nz * nxy
    rows, cols = proj_weight.shape
    own_tokens, depth = tokens.shape

    slab = lax.all_gather(tokens, (ZL, C), axis=0, tiled=True)
    slab_len = slab.shape[0]
    following = lax.ppermute(
        cotangent[: TAPS - 1], (ZH, X, Y), [(source, source - 1) for source in range(1, ndp)]
    )
    extended = jnp.concatenate([cotangent, following], 0).astype(F32)
    grad_feat = jnp.zeros((slab_len, cols), F32)
    for tap in range(TAPS):
        grad_feat = grad_feat + filters[tap] * extended[tap : tap + slab_len]
    grad_bf = grad_feat.astype(BF)

    weight = weight_columns(proj_weight)

    core = lax.axis_index(C)
    by_core = grad_bf.reshape(nzl, 2, own_tokens, cols)
    theirs = lax.dynamic_index_in_dim(by_core, 1 - core, 1, keepdims=False).reshape(-1, cols)
    ours = lax.dynamic_index_in_dim(by_core, core, 1, keepdims=False).reshape(-1, cols)
    contract_cols = (((1,), (1,)), ((), ()))
    for_other = lax.dot_general(theirs, weight, contract_cols, preferred_element_type=F32).astype(BF)
    from_other = lax.ppermute(for_other, C, [(0, 1), (1, 0)])
    here = lax.dot_general(ours, weight, contract_cols, preferred_element_type=F32)
    chip_sum = (here + from_other.astype(F32)).astype(BF)
    input_grad = lax.psum_scatter(chip_sum, ZL, scatter_dimension=0, tiled=True)

    partial = lax.dot_general(
        slab, grad_bf, (((0,), (0,)), ((), ())), preferred_element_type=F32
    ).astype(BF)
    partial = partial.reshape(nz, nxy, rows, cols).transpose(1, 0, 2, 3).reshape(nxy, nz * rows, cols)
    featured = jnp.dot(slab, weight, preferred_element_type=F32).astype(BF).astype(F32)
    taps = jnp.stack(
        [jnp.sum(featured * extended[tap : tap + slab_len], axis=0) for tap in range(TAPS)]
        + [jnp.zeros((cols,), F32)]
    )
    high = taps.astype(BF)
    low = (taps - high.astype(F32)).astype(BF)
    tail = jnp.broadcast_to(jnp.concatenate([high, low], 0)[None], (nxy, 16, cols))
    packed = jnp.concatenate([partial, tail], 1)
    arrived = lax.all_to_all(packed, (X, Y), split_axis=0, concat_axis=0, tiled=True)
    column_sum = jnp.sum(arrived.astype(F32), axis=0)
    body_rows = column_sum[: nz * rows]
    tap_rows = column_sum[nz * rows : nz * rows + 8] + column_sum[nz * rows + 8 :]
    total = lax.psum(jnp.concatenate([body_rows, tap_rows], 0), ZH)
    weight_grad = lax.dynamic_slice_in_dim(total, lax.axis_index(ZH) * rows, rows, 0).astype(BF)
    filter_grad = total[nz * rows : nz * rows + TAPS]
    return input_grad, weight_grad, filter_grad


def solution(mesh):
    fine = Mesh(mesh.devices.reshape(4, 4, 4, 4, 2), (ZH, X, Y, ZL, C))
    dp, seq = (ZH, X, Y), (ZL, C)
    in_specs = (P(dp + seq, None), P(dp, seq), P(dp, seq), P(None, seq))
    out_specs = (P(dp + seq, None), P(dp, seq), P(None, seq))
    return jax.shard_map(body, mesh=fine, in_specs=in_specs, out_specs=out_specs, check_vma=False)
```

```python
import jax
import jax.numpy as jnp
from jax import lax
from jax.sharding import Mesh, PartitionSpec as P

TAPS = 7
BF = jnp.bfloat16
F32 = jnp.float32
ZH, X, Y, ZL, C = "zh", "x", "y", "zl", "c"


def split_rows(value):
    high = value.astype(BF)
    return jnp.concatenate([high, (value - high.astype(F32)).astype(BF)], 0)


def joined_rows(value):
    half = value.shape[0] // 2
    return value[:half] + value[half:]


def weight_columns(proj_weight):
    rows, cols = proj_weight.shape
    nz = lax.axis_size(ZH)
    nxy = lax.axis_size((X, Y))
    column = lax.all_gather(proj_weight, ZH)
    repeated = jnp.broadcast_to(column[None], (nxy, nz, rows, cols))
    gathered = lax.all_to_all(repeated, (X, Y), split_axis=0, concat_axis=0, tiled=True)
    return gathered.transpose(1, 0, 2, 3).reshape(nz * nxy * rows, cols)


def body(tokens, proj_weight, cotangent, filters):
    nz = lax.axis_size(ZH)
    nxy = lax.axis_size((X, Y))
    nzl = lax.axis_size(ZL)
    ndp = nz * nxy
    rows, cols = proj_weight.shape
    own_tokens, depth = tokens.shape

    slab = lax.all_gather(tokens, (ZL, C), axis=0, tiled=True)
    slab_len = slab.shape[0]
    following = lax.ppermute(
        cotangent[: TAPS - 1], (ZH, X, Y), [(source, source - 1) for source in range(1, ndp)]
    )
    extended = jnp.concatenate([cotangent, following], 0).astype(F32)
    grad_feat = jnp.zeros((slab_len, cols), F32)
    for tap in range(TAPS):
        grad_feat = grad_feat + filters[tap] * extended[tap : tap + slab_len]
    grad_bf = grad_feat.astype(BF)

    weight = weight_columns(proj_weight)

    core = lax.axis_index(C)
    by_core = grad_bf.reshape(nzl, 2, own_tokens, cols)
    theirs = lax.dynamic_index_in_dim(by_core, 1 - core, 1, keepdims=False).reshape(-1, cols)
    ours = lax.dynamic_index_in_dim(by_core, core, 1, keepdims=False).reshape(-1, cols)
    contract_cols = (((1,), (1,)), ((), ()))
    for_other = lax.dot_general(theirs, weight, contract_cols, preferred_element_type=F32).astype(BF)
    from_other = lax.ppermute(for_other, C, [(0, 1), (1, 0)])
    here = lax.dot_general(ours, weight, contract_cols, preferred_element_type=F32)
    chip_sum = (here + from_other.astype(F32)).astype(BF)
    input_grad = lax.psum_scatter(chip_sum, ZL, scatter_dimension=0, tiled=True)

    partial = lax.dot_general(
        slab, grad_bf, (((0,), (0,)), ((), ())), preferred_element_type=F32
    ).astype(BF)
    partial = partial.reshape(nz, nxy, rows, cols).transpose(1, 0, 2, 3).reshape(nxy, nz * rows, cols)
    featured = jnp.dot(slab, weight, preferred_element_type=F32).astype(BF).astype(F32)
    taps = jnp.stack(
        [jnp.sum(featured * extended[tap : tap + slab_len], axis=0) for tap in range(TAPS)]
        + [jnp.zeros((cols,), F32)]
    )
    tail = jnp.broadcast_to(split_rows(taps)[None], (nxy, 16, cols))
    packed = jnp.concatenate([partial, tail], 1)
    arrived = lax.all_to_all(packed, (X, Y), split_axis=0, concat_axis=0, tiled=True)
    column_sum = jnp.sum(arrived.astype(F32), axis=0)
    blocks = column_sum[: nz * rows].astype(BF).reshape(nz, rows, cols)
    tail = jnp.broadcast_to(split_rows(joined_rows(column_sum[nz * rows :]))[None], (nz, 16, cols))
    packed = jnp.concatenate([blocks, tail], 1)
    arrived = lax.all_to_all(packed, ZH, split_axis=0, concat_axis=0, tiled=True)
    total = jnp.sum(arrived.astype(F32), axis=0)
    weight_grad = total[:rows].astype(BF)
    filter_grad = joined_rows(total[rows:])[:TAPS]
    return input_grad, weight_grad, filter_grad


def solution(mesh):
    fine = Mesh(mesh.devices.reshape(4, 4, 4, 4, 2), (ZH, X, Y, ZL, C))
    dp, seq = (ZH, X, Y), (ZL, C)
    in_specs = (P(dp + seq, None), P(dp, seq), P(dp, seq), P(None, seq))
    out_specs = (P(dp + seq, None), P(dp, seq), P(None, seq))
    return jax.shard_map(body, mesh=fine, in_specs=in_specs, out_specs=out_specs, check_vma=False)
```

```python
import jax
import jax.numpy as jnp
from jax import lax
from jax.sharding import Mesh, PartitionSpec as P

TAPS = 7
BF = jnp.bfloat16
F32 = jnp.float32
ZH, X, Y, ZL, C = "zh", "x", "y", "zl", "c"


def split_rows(value):
    high = value.astype(BF)
    return jnp.concatenate([high, (value - high.astype(F32)).astype(BF)], 0)


def joined_rows(value):
    half = value.shape[0] // 2
    return value[:half] + value[half:]


def exchange(value, axes):
    return lax.all_to_all(value, axes, split_axis=0, concat_axis=0, tiled=True)


def spread(value, axes):
    count = lax.axis_size(axes)
    return exchange(jnp.broadcast_to(value[None], (count,) + value.shape), axes)


def from_ahead(value, axis, steps):
    count = lax.axis_size(axis)
    return lax.ppermute(value, axis, [(source, (source - steps) % count) for source in range(count)])


def swap(value):
    return lax.ppermute(value, C, [(0, 1), (1, 0)])


def rolled(value, start):
    return lax.dynamic_slice_in_dim(jnp.concatenate([value, value], 0), start, value.shape[0], 0)


def body(tokens, proj_weight, cotangent, filters):
    nz = lax.axis_size(ZH)
    nxy = lax.axis_size((X, Y))
    nzl = lax.axis_size(ZL)
    ndp = nz * nxy
    rows, cols = proj_weight.shape
    own_tokens, depth = tokens.shape
    slab_len = cotangent.shape[0]
    core, chip = lax.axis_index(C), lax.axis_index(ZL)
    chip_tokens = 2 * own_tokens

    direct = [tokens] + [None] * (nzl - 1)
    for steps in (2, 1, 3):
        direct[steps] = from_ahead(tokens, ZL, steps)
    column = spread(proj_weight, ZH)
    following = lax.ppermute(
        cotangent[: TAPS - 1], (ZH, X, Y), [(source, source - 1) for source in range(1, ndp)]
    )
    crossed = [swap(value) for value in direct]
    parts = []
    for mine, other in zip(direct, crossed):
        parts += [jnp.where(core == 0, mine, other), jnp.where(core == 0, other, mine)]
    slab = jnp.concatenate(parts, 0)

    extended = jnp.concatenate([cotangent, following], 0).astype(F32)
    grad_feat = jnp.zeros((slab_len, cols), F32)
    for tap in range(TAPS):
        grad_feat = grad_feat + filters[tap] * extended[tap : tap + slab_len]
    grad_bf = grad_feat.astype(BF)

    gathered = spread(column.reshape(nz * rows, cols), (X, Y))
    weight = gathered.reshape(nxy, nz, rows, cols).transpose(1, 0, 2, 3).reshape(depth, cols)

    partial = lax.dot_general(
        slab, rolled(grad_bf, chip * chip_tokens), (((0,), (0,)), ((), ())), preferred_element_type=F32
    ).astype(BF)
    partial = partial.reshape(nz, nxy, rows, cols).transpose(1, 0, 2, 3).reshape(nxy, nz * rows, cols)
    arrived = exchange(partial, (X, Y))
    blocks = jnp.sum(arrived.astype(F32), axis=0).astype(BF).reshape(nz, rows, cols)

    by_core = grad_bf.reshape(nzl, 2, own_tokens, cols)
    theirs = lax.dynamic_index_in_dim(by_core, 1 - core, 1, keepdims=False).reshape(-1, cols)
    ours = lax.dynamic_index_in_dim(by_core, core, 1, keepdims=False).reshape(-1, cols)
    contract_cols = (((1,), (1,)), ((), ()))
    for_other = lax.dot_general(theirs, weight, contract_cols, preferred_element_type=F32).astype(BF)
    from_other = swap(for_other)
    here = lax.dot_general(ours, weight, contract_cols, preferred_element_type=F32)
    chip_sum = (here + from_other.astype(F32)).astype(BF).reshape(nzl, own_tokens, depth)
    total = lax.dynamic_index_in_dim(chip_sum, chip, 0, keepdims=False).astype(F32)
    for steps in (2, 1, 3):
        outgoing = lax.dynamic_index_in_dim(chip_sum, (chip - steps) % nzl, 0, keepdims=False)
        total = total + from_ahead(outgoing, ZL, steps).astype(F32)
    input_grad = total.astype(BF)

    featured = jnp.dot(slab, weight, preferred_element_type=F32).astype(BF)
    featured = rolled(featured, (nzl - chip) * chip_tokens).astype(F32)
    taps = jnp.stack(
        [jnp.sum(featured * extended[tap : tap + slab_len], axis=0) for tap in range(TAPS)]
        + [jnp.zeros((cols,), F32)]
    )
    taps = joined_rows(jnp.sum(spread(split_rows(taps), (X, Y)).reshape(nxy, 16, cols).astype(F32), axis=0))

    tail = jnp.broadcast_to(split_rows(taps)[None], (nz, 16, cols))
    arrived = exchange(jnp.concatenate([blocks, tail], 1), ZH)
    summed = jnp.sum(arrived.astype(F32), axis=0)
    weight_grad = summed[:rows].astype(BF)
    filter_grad = joined_rows(summed[rows:])[:TAPS]
    return input_grad, weight_grad, filter_grad


def solution(mesh):
    fine = Mesh(mesh.devices.reshape(4, 4, 4, 4, 2), (ZH, X, Y, ZL, C))
    dp, seq = (ZH, X, Y), (ZL, C)
    in_specs = (P(dp + seq, None), P(dp, seq), P(dp, seq), P(None, seq))
    out_specs = (P(dp + seq, None), P(dp, seq), P(None, seq))
    return jax.shard_map(body, mesh=fine, in_specs=in_specs, out_specs=out_specs, check_vma=False)
```

```python
import jax
import jax.numpy as jnp
from jax import lax
from jax.sharding import Mesh, PartitionSpec as P

TAPS = 7
BF = jnp.bfloat16
F32 = jnp.float32
ZH, X, Y, ZL, C = "zh", "x", "y", "zl", "c"


def split_rows(value):
    high = value.astype(BF)
    return jnp.concatenate([high, (value - high.astype(F32)).astype(BF)], 0)


def joined_rows(value):
    half = value.shape[0] // 2
    return value[:half] + value[half:]


def weight_columns(proj_weight):
    rows, cols = proj_weight.shape
    nz = lax.axis_size(ZH)
    nxy = lax.axis_size((X, Y))
    column = lax.all_gather(proj_weight, ZH)
    repeated = jnp.broadcast_to(column[None], (nxy, nz, rows, cols))
    gathered = lax.all_to_all(repeated, (X, Y), split_axis=0, concat_axis=0, tiled=True)
    return gathered.transpose(1, 0, 2, 3).reshape(nz * nxy * rows, cols)


def body(tokens, proj_weight, cotangent, filters):
    nz = lax.axis_size(ZH)
    nxy = lax.axis_size((X, Y))
    nzl = lax.axis_size(ZL)
    ndp = nz * nxy
    rows, cols = proj_weight.shape
    own_tokens, depth = tokens.shape

    slab = lax.all_gather(tokens, (ZL, C), axis=0, tiled=True)
    slab_len = slab.shape[0]
    following = lax.ppermute(
        cotangent[: TAPS - 1], (ZH, X, Y), [(source, source - 1) for source in range(1, ndp)]
    )
    extended = jnp.concatenate([cotangent, following], 0).astype(F32)
    grad_feat = jnp.zeros((slab_len, cols), F32)
    for tap in range(TAPS):
        grad_feat = grad_feat + filters[tap] * extended[tap : tap + slab_len]
    grad_bf = grad_feat.astype(BF)

    weight = weight_columns(proj_weight)

    core = lax.axis_index(C)
    by_core = grad_bf.reshape(nzl, 2, own_tokens, cols)
    theirs = lax.dynamic_index_in_dim(by_core, 1 - core, 1, keepdims=False).reshape(-1, cols)
    ours = lax.dynamic_index_in_dim(by_core, core, 1, keepdims=False).reshape(-1, cols)
    contract_cols = (((1,), (1,)), ((), ()))
    for_other = lax.dot_general(theirs, weight, contract_cols, preferred_element_type=F32).astype(BF)
    from_other = lax.ppermute(for_other, C, [(0, 1), (1, 0)])
    here = lax.dot_general(ours, weight, contract_cols, preferred_element_type=F32)
    chip_sum = (here + from_other.astype(F32)).astype(BF)

    chip_sum, grad_late = lax.optimization_barrier((chip_sum, grad_bf))
    input_grad = lax.psum_scatter(chip_sum, ZL, scatter_dimension=0, tiled=True)
    partial = lax.dot_general(
        slab, grad_late, (((0,), (0,)), ((), ())), preferred_element_type=F32
    ).astype(BF)
    partial = partial.reshape(nz, nxy, rows, cols).transpose(1, 0, 2, 3).reshape(nxy, nz * rows, cols)
    featured = jnp.dot(slab, weight, preferred_element_type=F32).astype(BF).astype(F32)
    taps = jnp.stack(
        [jnp.sum(featured * extended[tap : tap + slab_len], axis=0) for tap in range(TAPS)]
        + [jnp.zeros((cols,), F32)]
    )
    tail = jnp.broadcast_to(split_rows(taps)[None], (nxy, 16, cols))
    packed = jnp.concatenate([partial, tail], 1)
    arrived = lax.all_to_all(packed, (X, Y), split_axis=0, concat_axis=0, tiled=True)
    column_sum = jnp.sum(arrived.astype(F32), axis=0)
    blocks = column_sum[: nz * rows].astype(BF)
    tail = split_rows(joined_rows(column_sum[nz * rows :]))
    arrived = lax.all_gather(jnp.concatenate([blocks, tail], 0), ZH).astype(F32)
    total = jnp.sum(arrived, axis=0)
    weight_grad = lax.dynamic_slice_in_dim(total, lax.axis_index(ZH) * rows, rows, 0).astype(BF)
    filter_grad = joined_rows(total[nz * rows :])[:TAPS]
    return input_grad, weight_grad, filter_grad


def solution(mesh):
    fine = Mesh(mesh.devices.reshape(4, 4, 4, 4, 2), (ZH, X, Y, ZL, C))
    dp, seq = (ZH, X, Y), (ZL, C)
    in_specs = (P(dp + seq, None), P(dp, seq), P(dp, seq), P(None, seq))
    out_specs = (P(dp + seq, None), P(dp, seq), P(None, seq))
    return jax.shard_map(body, mesh=fine, in_specs=in_specs, out_specs=out_specs, check_vma=False)
```

```python
import jax
import jax.numpy as jnp
from jax import lax
from jax.sharding import Mesh, PartitionSpec as P

TAPS = 7
BF = jnp.bfloat16
F32 = jnp.float32
ZH, X, Y, ZP, ZQ, C = "zh", "x", "y", "zp", "zq", "c"
DP, SEQ, XY, PAIR, COLUMN = (ZH, X, Y), (ZP, ZQ, C), (X, Y), (ZQ, C), (ZH, ZQ, C)


def split_rows(value, parts):
    pieces = []
    for _ in range(parts):
        piece = value.astype(BF)
        pieces.append(piece)
        value = value - piece.astype(F32)
    return pieces


def exchange(value, axes):
    return lax.all_to_all(value, axes, split_axis=0, concat_axis=0, tiled=True)


def spread(value, axes):
    return exchange(jnp.broadcast_to(value[None], (lax.axis_size(axes),) + value.shape), axes)


def body(tokens, proj_weight, cotangent, filters):
    nz, nxy, nseq, npair = (lax.axis_size(a) for a in (ZH, XY, SEQ, PAIR))
    ndp = nz * nxy
    rows, cols = proj_weight.shape
    own_tokens, depth = tokens.shape
    slab_len = cotangent.shape[0]
    quarter, half = depth // npair, cols * npair
    zh, mine = lax.axis_index(ZH), lax.axis_index(PAIR)

    head = cotangent[: TAPS + 1]
    following = lax.ppermute(head, DP, [(source, source - 1) for source in range(1, ndp)])
    taps3 = [jnp.pad(piece, ((0, 1), (0, 0))) for piece in split_rows(filters, 3)]
    block = lax.all_gather(jnp.concatenate([cotangent, following] + taps3, 0), PAIR)
    block = block.transpose(1, 0, 2).reshape(-1, half).astype(F32)
    extended = block[: slab_len + TAPS + 1]
    taps = block[slab_len + TAPS + 1 :].reshape(3, TAPS + 1, half)
    taps = taps[0] + taps[1] + taps[2]

    column = spread(proj_weight, COLUMN).reshape(nz, npair, rows, cols)
    column = lax.dynamic_index_in_dim(column, mine, 0, keepdims=False)
    column = column.transpose(1, 0, 2).reshape(rows, half)
    weight = spread(column, XY).reshape(quarter, half)

    pieces = tokens.reshape(own_tokens, npair, quarter).transpose(1, 0, 2)
    pieces = jnp.broadcast_to(pieces[None], (nseq // npair,) + pieces.shape)
    slab = exchange(pieces.reshape(nseq, own_tokens, quarter), SEQ).reshape(slab_len, quarter)

    grad_feat = jnp.zeros((slab_len, half), F32)
    for tap in range(TAPS):
        grad_feat = grad_feat + taps[tap] * extended[tap : tap + slab_len]
    grad_bf = grad_feat.astype(BF)

    partial = lax.dot_general(grad_bf, weight, (((1,), (1,)), ((), ())), preferred_element_type=F32)
    arrived = exchange(partial.astype(BF).reshape(nseq, own_tokens, quarter), SEQ)
    arrived = arrived.reshape(nseq // npair, npair, own_tokens, quarter).astype(F32)
    input_grad = jnp.sum(arrived, axis=0).transpose(1, 0, 2).reshape(own_tokens, depth).astype(BF)

    products = lax.dot_general(slab, grad_bf, (((0,), (0,)), ((), ())), preferred_element_type=F32)
    featured = jnp.dot(slab, weight, preferred_element_type=F32)
    tap_sums = jnp.stack(
        [jnp.sum(featured * extended[tap : tap + slab_len], axis=0) for tap in range(TAPS)]
        + [jnp.zeros((half,), F32)]
    )
    tail = jnp.broadcast_to(jnp.concatenate(split_rows(tap_sums, 2), 0)[None], (nxy, 16, half))
    arrived = exchange(jnp.concatenate([products.astype(BF).reshape(nxy, rows, half), tail], 1), XY)
    summed = jnp.sum(arrived.astype(F32), axis=0)

    tap_sums = summed[rows : rows + 8] + summed[rows + 8 :]
    packed = jnp.concatenate([summed[:rows].astype(BF)] + split_rows(tap_sums, 2), 0)
    packed = packed.reshape(-1, npair, cols).transpose(1, 0, 2)
    packed = jnp.broadcast_to(packed[None], (nz,) + packed.shape).reshape(nz * npair, -1, cols)
    arrived = exchange(packed, COLUMN).reshape(nz, npair, -1, cols)
    blocks = lax.dynamic_index_in_dim(arrived, zh, 1, keepdims=False)[:, :rows]
    weight_grad = jnp.sum(blocks.astype(F32), axis=0).astype(BF)
    tails = jnp.sum(arrived[:, :, rows:].astype(F32), axis=(0, 1))
    filter_grad = tails[:TAPS] + tails[8 : 8 + TAPS]
    return input_grad, weight_grad, filter_grad


def solution(mesh):
    fine = Mesh(mesh.devices.reshape(4, 4, 4, 2, 2, 2), (ZH, X, Y, ZP, ZQ, C))
    in_specs = (P(DP + SEQ, None), P(DP, SEQ), P(DP, SEQ), P(None, SEQ))
    out_specs = (P(DP + SEQ, None), P(DP, SEQ), P(None, SEQ))
    return jax.shard_map(body, mesh=fine, in_specs=in_specs, out_specs=out_specs, check_vma=False)
```

```python
import jax
import jax.numpy as jnp
from jax import lax
from jax.experimental import pallas as pl
from jax.experimental.pallas import tpu as pltpu
from jax.sharding import Mesh, PartitionSpec as P

TAPS = 7
BF = jnp.bfloat16
F32 = jnp.float32
ZH, X, Y, ZL, C = "zh", "x", "y", "zl", "c"


def split_rows(value):
    high = value.astype(BF)
    return jnp.concatenate([high, (value - high.astype(F32)).astype(BF)], 0)


def joined_rows(value):
    half = value.shape[0] // 2
    return value[:half] + value[half:]


def exchange(value, axes):
    return lax.all_to_all(value, axes, split_axis=0, concat_axis=0, tiled=True)


def from_ahead(value, axis, steps):
    count = lax.axis_size(axis)
    return lax.ppermute(value, axis, [(source, (source - steps) % count) for source in range(count)])


def products_kernel(slab_ref, weight_ref, grad_ref, extended_ref, out_ref, featured_ref):
    step = pl.program_id(0)
    slab_len, cols = grad_ref.shape
    nxy = out_ref.shape[0]
    rows = slab_ref.shape[1] // nxy
    products = lax.dot_general(
        slab_ref[...], grad_ref[...], (((0,), (0,)), ((), ())), preferred_element_type=F32
    )
    here = pl.ds(pl.multiple_of(step * rows, rows), rows)
    out_ref[:, here, :] = products.astype(BF).reshape(nxy, rows, cols)
    term = jnp.dot(slab_ref[...], weight_ref[...], preferred_element_type=F32)

    @pl.when(step == 0)
    def _():
        featured_ref[...] = term

    @pl.when(step > 0)
    def _():
        featured_ref[...] += term

    @pl.when(step == pl.num_programs(0) - 1)
    def _():
        featured = featured_ref[...].astype(BF).astype(F32)
        sums = [
            jnp.sum(featured * extended_ref[tap : tap + slab_len, :], axis=0, keepdims=True)
            for tap in range(TAPS)
        ]
        tail = split_rows(jnp.concatenate(sums + [jnp.zeros((1, cols), F32)], 0))
        out_ref[:, pl.num_programs(0) * rows :, :] = jnp.broadcast_to(tail[None], (nxy, 16, cols))


def local_products(slab, weight, grad_bf, extended, nxy, rows):
    slab_len, depth = slab.shape
    cols = weight.shape[1]
    nz = depth // (nxy * rows)
    part = nxy * rows
    return pl.pallas_call(
        products_kernel,
        grid=(nz,),
        in_specs=[
            pl.BlockSpec((slab_len, part), lambda i: (0, i)),
            pl.BlockSpec((part, cols), lambda i: (i, 0)),
            pl.BlockSpec((slab_len, cols), lambda i: (0, 0)),
            pl.BlockSpec(extended.shape, lambda i: (0, 0)),
        ],
        out_specs=pl.BlockSpec((nxy, nz * rows + 16, cols), lambda i: (0, 0, 0)),
        out_shape=jax.ShapeDtypeStruct((nxy, nz * rows + 16, cols), BF),
        scratch_shapes=[pltpu.VMEM((slab_len, cols), F32)],
        compiler_params=pltpu.CompilerParams(vmem_limit_bytes=32 * 1024 * 1024),
        cost_estimate=pl.CostEstimate(
            flops=4 * slab_len * depth * cols, bytes_accessed=4 * slab_len * depth, transcendentals=0
        ),
    )(slab, weight, grad_bf, extended)


def weight_columns(proj_weight):
    rows, cols = proj_weight.shape
    nz = lax.axis_size(ZH)
    nxy = lax.axis_size((X, Y))
    column = lax.all_gather(proj_weight, ZH)
    repeated = jnp.broadcast_to(column[None], (nxy, nz, rows, cols))
    gathered = lax.all_to_all(repeated, (X, Y), split_axis=0, concat_axis=0, tiled=True)
    return gathered.transpose(1, 0, 2, 3).reshape(nz * nxy * rows, cols)


def body(tokens, proj_weight, cotangent, filters):
    nz = lax.axis_size(ZH)
    nxy = lax.axis_size((X, Y))
    nzl = lax.axis_size(ZL)
    ndp = nz * nxy
    rows, cols = proj_weight.shape
    own_tokens, depth = tokens.shape

    slab = lax.all_gather(tokens, (ZL, C), axis=0, tiled=True)
    slab_len = slab.shape[0]
    following = lax.ppermute(
        cotangent[: TAPS - 1], (ZH, X, Y), [(source, source - 1) for source in range(1, ndp)]
    )
    nothing = jnp.zeros((2, cols), BF)
    extended = jnp.concatenate([cotangent, following, nothing], 0).astype(F32)
    grad_feat = jnp.zeros((slab_len, cols), F32)
    for tap in range(TAPS):
        grad_feat = grad_feat + filters[tap] * extended[tap : tap + slab_len]
    grad_bf = grad_feat.astype(BF)

    weight = weight_columns(proj_weight)

    core, chip = lax.axis_index(C), lax.axis_index(ZL)
    by_core = grad_bf.reshape(nzl, 2, own_tokens, cols)
    theirs = lax.dynamic_index_in_dim(by_core, 1 - core, 1, keepdims=False).reshape(-1, cols)
    ours = lax.dynamic_index_in_dim(by_core, core, 1, keepdims=False).reshape(-1, cols)
    contract_cols = (((1,), (1,)), ((), ()))
    for_other = lax.dot_general(theirs, weight, contract_cols, preferred_element_type=F32).astype(BF)
    for_other, grad_late = lax.optimization_barrier((for_other, grad_bf))
    from_other = lax.ppermute(for_other, C, [(0, 1), (1, 0)])

    packed = local_products(slab, weight, grad_late, extended, nxy, rows)
    packed, ours = lax.optimization_barrier((packed, ours))
    arrived = exchange(packed, (X, Y))
    total = jnp.sum(arrived.astype(F32), axis=0)

    here = lax.dot_general(ours, weight, contract_cols, preferred_element_type=F32)
    chip_sum = (here + from_other.astype(F32)).astype(BF)
    chip_sum = chip_sum.reshape(nzl, own_tokens, depth)
    summed = lax.dynamic_index_in_dim(chip_sum, chip, 0, keepdims=False).astype(F32)
    for steps in (2, 1, 3):
        outgoing = lax.dynamic_index_in_dim(chip_sum, (chip - steps) % nzl, 0, keepdims=False)
        summed = summed + from_ahead(outgoing, ZL, steps).astype(F32)
    input_grad = summed.astype(BF)

    blocks = total[: nz * rows].astype(BF).reshape(nz, rows, cols)
    tail = split_rows(joined_rows(total[nz * rows :]))
    packed = jnp.concatenate([blocks, jnp.broadcast_to(tail[None], (nz, 16, cols))], 1)
    arrived = exchange(packed, ZH)
    arrived, input_grad = lax.optimization_barrier((arrived, input_grad))
    total = jnp.sum(arrived.astype(F32), axis=0)
    weight_grad = total[:rows].astype(BF)
    filter_grad = joined_rows(total[rows:])[:TAPS]
    return input_grad, weight_grad, filter_grad


def solution(mesh):
    fine = Mesh(mesh.devices.reshape(4, 4, 4, 4, 2), (ZH, X, Y, ZL, C))
    dp, seq = (ZH, X, Y), (ZL, C)
    in_specs = (P(dp + seq, None), P(dp, seq), P(dp, seq), P(None, seq))
    out_specs = (P(dp + seq, None), P(dp, seq), P(None, seq))
    return jax.shard_map(body, mesh=fine, in_specs=in_specs, out_specs=out_specs, check_vma=False)
```

```python
import jax
import jax.numpy as jnp
from jax import lax
from jax.experimental import pallas as pl
from jax.experimental.pallas import tpu as pltpu
from jax.sharding import Mesh, PartitionSpec as P

TAPS = 7
VMEM_BYTES = 12 * 1024 * 1024
BF = jnp.bfloat16
F32 = jnp.float32
ZH, X, Y, ZL, C = "zh", "x", "y", "zl", "c"


def split_rows(value):
    high = value.astype(BF)
    return jnp.concatenate([high, (value - high.astype(F32)).astype(BF)], 0)


def joined_rows(value):
    half = value.shape[0] // 2
    return value[:half] + value[half:]


def exchange(value, axes):
    return lax.all_to_all(value, axes, split_axis=0, concat_axis=0, tiled=True)


def from_ahead(value, axis, steps):
    count = lax.axis_size(axis)
    return lax.ppermute(value, axis, [(source, (source - steps) % count) for source in range(count)])


def in_order(place_ref, chunks, block_ref):
    count = chunks[0].shape[0]
    for index, chunk in enumerate(chunks):
        block_ref[pl.ds(pl.multiple_of(place_ref[index] * count, count), count), :] = chunk[...]


def products_kernel(place_ref, *refs):
    chunks, (grad_ref, out_ref, block_ref) = refs[:-3], refs[-3:]
    nxy, cols = out_ref.shape[0], grad_ref.shape[1]
    rows = chunks[0].shape[1] // nxy
    in_order(place_ref, chunks, block_ref)
    products = lax.dot_general(
        block_ref[...], grad_ref[...], (((0,), (0,)), ((), ())), preferred_element_type=F32
    )
    here = pl.ds(pl.multiple_of(pl.program_id(0) * rows, rows), rows)
    out_ref[:, here, :] = products.astype(BF).reshape(nxy, rows, cols)

    @pl.when(pl.program_id(0) == 0)
    def _():
        out_ref[:, pl.num_programs(0) * rows :, :] = jnp.zeros((nxy, 16, cols), BF)


def weight_products(places, chunks, grad_bf, nxy, rows):
    slab_len, cols = grad_bf.shape
    step_rows, depth = chunks[0].shape
    part = nxy * rows
    nz = depth // part
    return pl.pallas_call(
        products_kernel,
        grid_spec=pltpu.PrefetchScalarGridSpec(
            num_scalar_prefetch=1,
            grid=(nz,),
            in_specs=[pl.BlockSpec((step_rows, part), lambda i, _: (0, i)) for _ in chunks]
            + [pl.BlockSpec((slab_len, cols), lambda i, _: (0, 0))],
            out_specs=pl.BlockSpec((nxy, nz * rows + 16, cols), lambda i, _: (0, 0, 0)),
            scratch_shapes=[pltpu.VMEM((slab_len, part), BF)],
        ),
        out_shape=jax.ShapeDtypeStruct((nxy, nz * rows + 16, cols), BF),
        compiler_params=pltpu.CompilerParams(vmem_limit_bytes=VMEM_BYTES),
        cost_estimate=pl.CostEstimate(
            flops=2 * slab_len * depth * cols, bytes_accessed=6 * slab_len * depth, transcendentals=0
        ),
    )(places, *chunks, grad_bf)


def taps_kernel(place_ref, *refs):
    chunks, (weight_ref, extended_ref, _, out_ref, block_ref, featured_ref) = refs[:-6], refs[-6:]
    step = pl.program_id(0)
    slab_len, cols = featured_ref.shape
    in_order(place_ref, chunks, block_ref)
    term = jnp.dot(block_ref[...], weight_ref[...], preferred_element_type=F32)

    @pl.when(step == 0)
    def _():
        featured_ref[...] = term

    @pl.when(step > 0)
    def _():
        featured_ref[...] += term

    @pl.when(step == pl.num_programs(0) - 1)
    def _():
        featured = featured_ref[...].astype(BF).astype(F32)
        sums = [
            jnp.sum(featured * extended_ref[tap : tap + slab_len, :], axis=0, keepdims=True)
            for tap in range(TAPS)
        ]
        tail = split_rows(jnp.concatenate(sums + [jnp.zeros((1, cols), F32)], 0))
        out_ref[...] = jnp.broadcast_to(tail[None], out_ref.shape)


def with_tap_sums(packed, places, chunks, weight, extended):
    step_rows, depth = chunks[0].shape
    slab_len, cols = step_rows * len(chunks), weight.shape[1]
    steps = 4
    part = depth // steps
    nxy, packed_rows, _ = packed.shape
    last = packed_rows // 16 - 1
    return pl.pallas_call(
        taps_kernel,
        grid_spec=pltpu.PrefetchScalarGridSpec(
            num_scalar_prefetch=1,
            grid=(steps,),
            in_specs=[pl.BlockSpec((step_rows, part), lambda i, _: (0, i)) for _ in chunks]
            + [
                pl.BlockSpec((part, cols), lambda i, _: (i, 0)),
                pl.BlockSpec(extended.shape, lambda i, _: (0, 0)),
                pl.BlockSpec((1, 16, cols), lambda i, _: (0, last, 0)),
            ],
            out_specs=pl.BlockSpec((nxy, 16, cols), lambda i, _: (0, last, 0)),
            scratch_shapes=[pltpu.VMEM((slab_len, part), BF), pltpu.VMEM((slab_len, cols), F32)],
        ),
        out_shape=jax.ShapeDtypeStruct(packed.shape, BF),
        input_output_aliases={len(chunks) + 3: 0},
        compiler_params=pltpu.CompilerParams(vmem_limit_bytes=VMEM_BYTES),
        cost_estimate=pl.CostEstimate(
            flops=2 * slab_len * depth * cols, bytes_accessed=3 * slab_len * depth, transcendentals=0
        ),
    )(places, *chunks, weight, extended, packed)


def spread(value, axes):
    return exchange(jnp.broadcast_to(value[None], (lax.axis_size(axes),) + value.shape), axes)


def swap(value):
    return lax.ppermute(value, C, [(0, 1), (1, 0)])


def weight_columns(proj_weight):
    rows, cols = proj_weight.shape
    nz, nxy = lax.axis_size(ZH), lax.axis_size((X, Y))
    gathered = spread(spread(proj_weight, ZH).reshape(nz * rows, cols), (X, Y))
    return gathered.reshape(nxy, nz, rows, cols).transpose(1, 0, 2, 3).reshape(nz * nxy * rows, cols)


def body(tokens, proj_weight, cotangent, filters):
    nz = lax.axis_size(ZH)
    nxy = lax.axis_size((X, Y))
    nzl = lax.axis_size(ZL)
    ndp = nz * nxy
    rows, cols = proj_weight.shape
    own_tokens, depth = tokens.shape

    slab_len = cotangent.shape[0]
    core, chip = lax.axis_index(C), lax.axis_index(ZL)
    direct = [tokens] + [None] * (nzl - 1)
    for steps in (2, 1, 3):
        direct[steps] = from_ahead(tokens, ZL, steps)
    sources = (chip + jnp.arange(nzl)) % nzl
    places = jnp.concatenate([2 * sources + core, 2 * sources + 1 - core]).astype(jnp.int32)
    following = lax.ppermute(
        cotangent[: TAPS - 1], (ZH, X, Y), [(source, source - 1) for source in range(1, ndp)]
    )
    nothing = jnp.zeros((2, cols), BF)
    extended = jnp.concatenate([cotangent, following, nothing], 0).astype(F32)
    grad_feat = jnp.zeros((slab_len, cols), F32)
    for tap in range(TAPS):
        grad_feat = grad_feat + filters[tap] * extended[tap : tap + slab_len]
    grad_bf = grad_feat.astype(BF)

    weight = weight_columns(proj_weight)
    chunks = direct + [swap(value) for value in direct]
    packed = weight_products(places, chunks, grad_bf, nxy, rows)
    packed = with_tap_sums(packed, places, chunks, weight, extended)
    packed, grad_late = lax.optimization_barrier((packed, grad_bf))
    total = jnp.sum(exchange(packed, (X, Y)).astype(F32), axis=0)

    by_core = grad_late.reshape(nzl, 2, own_tokens, cols)
    theirs = lax.dynamic_index_in_dim(by_core, 1 - core, 1, keepdims=False).reshape(-1, cols)
    ours = lax.dynamic_index_in_dim(by_core, core, 1, keepdims=False).reshape(-1, cols)
    contract_cols = (((1,), (1,)), ((), ()))
    for_other = lax.dot_general(theirs, weight, contract_cols, preferred_element_type=F32).astype(BF)
    from_other = swap(for_other)
    here = lax.dot_general(ours, weight, contract_cols, preferred_element_type=F32)
    chip_sum = (here + from_other.astype(F32)).astype(BF)
    chip_sum = chip_sum.reshape(nzl, own_tokens, depth)
    summed = lax.dynamic_index_in_dim(chip_sum, chip, 0, keepdims=False).astype(F32)
    for steps in (2, 1, 3):
        outgoing = lax.dynamic_index_in_dim(chip_sum, (chip - steps) % nzl, 0, keepdims=False)
        summed = summed + from_ahead(outgoing, ZL, steps).astype(F32)
    input_grad = summed.astype(BF)

    blocks = total[: nz * rows].astype(BF).reshape(nz, rows, cols)
    tail = split_rows(joined_rows(total[nz * rows :]))
    packed = jnp.concatenate([blocks, jnp.broadcast_to(tail[None], (nz, 16, cols))], 1)
    arrived = exchange(packed, ZH)
    arrived, input_grad = lax.optimization_barrier((arrived, input_grad))
    total = jnp.sum(arrived.astype(F32), axis=0)
    weight_grad = total[:rows].astype(BF)
    filter_grad = joined_rows(total[rows:])[:TAPS]
    return input_grad, weight_grad, filter_grad


def solution(mesh):
    fine = Mesh(mesh.devices.reshape(4, 4, 4, 4, 2), (ZH, X, Y, ZL, C))
    dp, seq = (ZH, X, Y), (ZL, C)
    in_specs = (P(dp + seq, None), P(dp, seq), P(dp, seq), P(None, seq))
    out_specs = (P(dp + seq, None), P(dp, seq), P(None, seq))
    return jax.shard_map(body, mesh=fine, in_specs=in_specs, out_specs=out_specs, check_vma=False)
```

```python
import jax
import jax.numpy as jnp
from jax import lax
from jax.experimental import pallas as pl
from jax.experimental.pallas import tpu as pltpu
from jax.sharding import Mesh, PartitionSpec as P

TAPS = 7
VMEM_BYTES = 12 * 1024 * 1024
BF = jnp.bfloat16
F32 = jnp.float32
ZH, X, Y, ZL, C = "zh", "x", "y", "zl", "c"


def split_rows(value):
    high = value.astype(BF)
    return jnp.concatenate([high, (value - high.astype(F32)).astype(BF)], 0)


def joined_rows(value):
    half = value.shape[0] // 2
    return value[:half] + value[half:]


def exchange(value, axes):
    return lax.all_to_all(value, axes, split_axis=0, concat_axis=0, tiled=True)


def from_ahead(value, axis, steps):
    count = lax.axis_size(axis)
    return lax.ppermute(value, axis, [(source, (source - steps) % count) for source in range(count)])


def in_order(place_ref, chunks, block_ref):
    count = chunks[0].shape[0]
    for index, chunk in enumerate(chunks):
        block_ref[pl.ds(pl.multiple_of(place_ref[index] * count, count), count), :] = chunk[...]


def products_kernel(place_ref, *refs):
    chunks, (grad_ref, out_ref, slab_ref) = refs[:-3], refs[-3:]
    nxy, cols = out_ref.shape[0], grad_ref.shape[1]
    rows = chunks[0].shape[1] // nxy
    in_order(place_ref, chunks, slab_ref)
    products = lax.dot_general(
        slab_ref[...], grad_ref[...], (((0,), (0,)), ((), ())), preferred_element_type=F32
    )
    here = pl.ds(pl.multiple_of(pl.program_id(0) * rows, rows), rows)
    out_ref[:, here, :] = products.astype(BF).reshape(nxy, rows, cols)

    @pl.when(pl.program_id(0) == 0)
    def _():
        out_ref[:, pl.num_programs(0) * rows :, :] = jnp.zeros((nxy, 16, cols), BF)


def weight_products(places, chunks, grad_bf, nxy, rows):
    slab_len, cols = grad_bf.shape
    step_rows, depth = chunks[0].shape
    part = nxy * rows
    nz = depth // part
    return pl.pallas_call(
        products_kernel,
        grid_spec=pltpu.PrefetchScalarGridSpec(
            num_scalar_prefetch=1,
            grid=(nz,),
            in_specs=[pl.BlockSpec((step_rows, part), lambda i, _: (0, i)) for _ in chunks]
            + [pl.BlockSpec((slab_len, cols), lambda i, _: (0, 0))],
            out_specs=[
                pl.BlockSpec((nxy, nz * rows + 16, cols), lambda i, _: (0, 0, 0)),
                pl.BlockSpec((slab_len, part), lambda i, _: (0, i)),
            ],
        ),
        out_shape=[
            jax.ShapeDtypeStruct((nxy, nz * rows + 16, cols), BF),
            jax.ShapeDtypeStruct((slab_len, depth), BF),
        ],
        compiler_params=pltpu.CompilerParams(vmem_limit_bytes=VMEM_BYTES),
        cost_estimate=pl.CostEstimate(
            flops=2 * slab_len * depth * cols, bytes_accessed=6 * slab_len * depth, transcendentals=0
        ),
    )(places, *chunks, grad_bf)


def taps_kernel(slab_ref, weight_ref, extended_ref, _, out_ref, featured_ref):
    step = pl.program_id(0)
    slab_len, cols = featured_ref.shape
    weight = weight_ref[...].reshape(-1, cols)
    term = jnp.dot(slab_ref[...], weight, preferred_element_type=F32)

    @pl.when(step == 0)
    def _():
        featured_ref[...] = term

    @pl.when(step > 0)
    def _():
        featured_ref[...] += term

    @pl.when(step == pl.num_programs(0) - 1)
    def _():
        featured = featured_ref[...].astype(BF).astype(F32)
        sums = [
            jnp.sum(featured * extended_ref[tap : tap + slab_len, :], axis=0, keepdims=True)
            for tap in range(TAPS)
        ]
        tail = split_rows(jnp.concatenate(sums + [jnp.zeros((1, cols), F32)], 0))
        out_ref[...] = jnp.broadcast_to(tail[None], out_ref.shape)


def with_tap_sums(packed, slab, gathered, extended):
    slab_len, depth = slab.shape
    nxy, nz, rows, cols = gathered.shape
    part = depth // nz
    last = packed.shape[1] // 16 - 1
    return pl.pallas_call(
        taps_kernel,
        grid=(nz,),
        in_specs=[
            pl.BlockSpec((slab_len, part), lambda i: (0, i)),
            pl.BlockSpec((nxy, 1, rows, cols), lambda i: (0, i, 0, 0)),
            pl.BlockSpec(extended.shape, lambda i: (0, 0)),
            pl.BlockSpec((1, 16, cols), lambda i: (0, last, 0)),
        ],
        out_specs=pl.BlockSpec((nxy, 16, cols), lambda i: (0, last, 0)),
        scratch_shapes=[pltpu.VMEM((slab_len, cols), F32)],
        out_shape=jax.ShapeDtypeStruct(packed.shape, BF),
        input_output_aliases={3: 0},
        compiler_params=pltpu.CompilerParams(vmem_limit_bytes=52 * 1024 * 1024),
        cost_estimate=pl.CostEstimate(
            flops=2 * slab_len * depth * cols, bytes_accessed=3 * slab_len * depth, transcendentals=0
        ),
    )(slab, gathered, extended, packed)


def spread(value, axes):
    return exchange(jnp.broadcast_to(value[None], (lax.axis_size(axes),) + value.shape), axes)


def swap(value):
    return lax.ppermute(value, C, [(0, 1), (1, 0)])


def body(tokens, proj_weight, cotangent, filters):
    nz = lax.axis_size(ZH)
    nxy = lax.axis_size((X, Y))
    nzl = lax.axis_size(ZL)
    ndp = nz * nxy
    rows, cols = proj_weight.shape
    own_tokens, depth = tokens.shape

    slab_len = cotangent.shape[0]
    core, chip = lax.axis_index(C), lax.axis_index(ZL)
    direct = [tokens] + [None] * (nzl - 1)
    for steps in (2, 1, 3):
        direct[steps] = from_ahead(tokens, ZL, steps)
    sources = (chip + jnp.arange(nzl)) % nzl
    places = jnp.concatenate([2 * sources + core, 2 * sources + 1 - core]).astype(jnp.int32)
    column = spread(proj_weight, ZH).reshape(nz * rows, cols)
    column, head = lax.optimization_barrier((column, cotangent[: TAPS - 1]))
    gathered = spread(column, (X, Y)).reshape(nxy, nz, rows, cols)
    following = lax.ppermute(
        head, (ZH, X, Y), [(source, source - 1) for source in range(1, ndp)]
    )
    nothing = jnp.zeros((2, cols), BF)
    extended = jnp.concatenate([cotangent, following, nothing], 0).astype(F32)
    grad_feat = jnp.zeros((slab_len, cols), F32)
    for tap in range(TAPS):
        grad_feat = grad_feat + filters[tap] * extended[tap : tap + slab_len]
    grad_bf = grad_feat.astype(BF)

    chunks = direct + [swap(value) for value in direct]
    packed, slab = weight_products(places, chunks, grad_bf, nxy, rows)
    packed = with_tap_sums(packed, slab, gathered, extended)
    packed, grad_late, gathered = lax.optimization_barrier((packed, grad_bf, gathered))
    total = jnp.sum(exchange(packed, (X, Y)).astype(F32), axis=0)

    weight = gathered.transpose(1, 0, 2, 3).reshape(depth, cols)
    by_core = grad_late.reshape(nzl, 2, own_tokens, cols)
    theirs = lax.dynamic_index_in_dim(by_core, 1 - core, 1, keepdims=False).reshape(-1, cols)
    ours = lax.dynamic_index_in_dim(by_core, core, 1, keepdims=False).reshape(-1, cols)
    contract_cols = (((1,), (1,)), ((), ()))
    for_other = lax.dot_general(theirs, weight, contract_cols, preferred_element_type=F32).astype(BF)
    from_other = swap(for_other)
    here = lax.dot_general(ours, weight, contract_cols, preferred_element_type=F32)
    chip_sum = (here + from_other.astype(F32)).astype(BF)
    chip_sum = chip_sum.reshape(nzl, own_tokens, depth)
    summed = lax.dynamic_index_in_dim(chip_sum, chip, 0, keepdims=False).astype(F32)
    for steps in (2, 1, 3):
        outgoing = lax.dynamic_index_in_dim(chip_sum, (chip - steps) % nzl, 0, keepdims=False)
        summed = summed + from_ahead(outgoing, ZL, steps).astype(F32)
    input_grad = summed.astype(BF)

    blocks = total[: nz * rows].astype(BF).reshape(nz, rows, cols)
    tail = split_rows(joined_rows(total[nz * rows :]))
    packed = jnp.concatenate([blocks, jnp.broadcast_to(tail[None], (nz, 16, cols))], 1)
    arrived = exchange(packed, ZH)
    arrived, input_grad = lax.optimization_barrier((arrived, input_grad))
    total = jnp.sum(arrived.astype(F32), axis=0)
    weight_grad = total[:rows].astype(BF)
    filter_grad = joined_rows(total[rows:])[:TAPS]
    return input_grad, weight_grad, filter_grad


def solution(mesh):
    fine = Mesh(mesh.devices.reshape(4, 4, 4, 4, 2), (ZH, X, Y, ZL, C))
    dp, seq = (ZH, X, Y), (ZL, C)
    in_specs = (P(dp + seq, None), P(dp, seq), P(dp, seq), P(None, seq))
    out_specs = (P(dp + seq, None), P(dp, seq), P(None, seq))
    return jax.shard_map(body, mesh=fine, in_specs=in_specs, out_specs=out_specs, check_vma=False)
```

```python
import jax
import jax.numpy as jnp
from jax import lax
from jax.experimental import pallas as pl
from jax.experimental.pallas import tpu as pltpu
from jax.sharding import Mesh, PartitionSpec as P

TAPS = 7
VMEM_BYTES = 12 * 1024 * 1024
BF = jnp.bfloat16
F32 = jnp.float32
ZH, X, Y, ZL, C = "zh", "x", "y", "zl", "c"


def split_rows(value):
    high = value.astype(BF)
    return jnp.concatenate([high, (value - high.astype(F32)).astype(BF)], 0)


def joined_rows(value):
    half = value.shape[0] // 2
    return value[:half] + value[half:]


def exchange(value, axes):
    return lax.all_to_all(value, axes, split_axis=0, concat_axis=0, tiled=True)


def from_ahead(value, axis, steps):
    count = lax.axis_size(axis)
    return lax.ppermute(value, axis, [(source, (source - steps) % count) for source in range(count)])


def order_kernel(place_ref, *refs):
    chunks, slab_ref = refs[:-1], refs[-1]
    count = chunks[0].shape[0]
    for index, chunk in enumerate(chunks):
        slab_ref[pl.ds(pl.multiple_of(place_ref[index] * count, count), count), :] = chunk[...]


def in_order(places, chunks):
    count, depth = chunks[0].shape
    part = depth // 4
    return pl.pallas_call(
        order_kernel,
        grid_spec=pltpu.PrefetchScalarGridSpec(
            num_scalar_prefetch=1,
            grid=(depth // part,),
            in_specs=[pl.BlockSpec((count, part), lambda i, _: (0, i)) for _ in chunks],
            out_specs=pl.BlockSpec((len(chunks) * count, part), lambda i, _: (0, i)),
        ),
        out_shape=jax.ShapeDtypeStruct((len(chunks) * count, depth), BF),
        compiler_params=pltpu.CompilerParams(vmem_limit_bytes=VMEM_BYTES),
        cost_estimate=pl.CostEstimate(
            flops=8 * 10**9, bytes_accessed=4 * len(chunks) * count * depth, transcendentals=0
        ),
    )(places, *chunks)


def products_kernel(slab_ref, weight_ref, grad_ref, extended_ref, out_ref, featured_ref):
    step = pl.program_id(0)
    slab_len, cols = grad_ref.shape
    nxy, rows, _ = weight_ref.shape
    products = lax.dot_general(
        slab_ref[...], grad_ref[...], (((0,), (0,)), ((), ())), preferred_element_type=F32
    )
    here = pl.ds(pl.multiple_of(step * rows, rows), rows)
    out_ref[:, here, :] = products.astype(BF).reshape(nxy, rows, cols)
    weight = weight_ref[...].reshape(nxy * rows, cols)
    term = jnp.dot(slab_ref[...], weight, preferred_element_type=F32)

    @pl.when(step == 0)
    def _():
        featured_ref[...] = term

    @pl.when(step > 0)
    def _():
        featured_ref[...] += term

    @pl.when(step == pl.num_programs(0) - 1)
    def _():
        featured = featured_ref[...].astype(BF).astype(F32)
        sums = [
            jnp.sum(featured * extended_ref[tap : tap + slab_len, :], axis=0, keepdims=True)
            for tap in range(TAPS)
        ]
        tail = split_rows(jnp.concatenate(sums + [jnp.zeros((1, cols), F32)], 0))
        out_ref[:, pl.num_programs(0) * rows :, :] = jnp.broadcast_to(tail[None], (nxy, 16, cols))


def local_products(slab, gathered, grad_bf, extended, nz, rows):
    slab_len, depth = slab.shape
    nxy, _, cols = gathered.shape
    part = nxy * rows
    return pl.pallas_call(
        products_kernel,
        grid=(nz,),
        in_specs=[
            pl.BlockSpec((slab_len, part), lambda i: (0, i)),
            pl.BlockSpec((nxy, rows, cols), lambda i: (0, i, 0)),
            pl.BlockSpec((slab_len, cols), lambda i: (0, 0)),
            pl.BlockSpec(extended.shape, lambda i: (0, 0)),
        ],
        out_specs=pl.BlockSpec((nxy, nz * rows + 16, cols), lambda i: (0, 0, 0)),
        out_shape=jax.ShapeDtypeStruct((nxy, nz * rows + 16, cols), BF),
        scratch_shapes=[pltpu.VMEM((slab_len, cols), F32)],
        compiler_params=pltpu.CompilerParams(vmem_limit_bytes=52 * 1024 * 1024),
        cost_estimate=pl.CostEstimate(
            flops=4 * slab_len * depth * cols, bytes_accessed=4 * slab_len * depth, transcendentals=0
        ),
    )(slab, gathered, grad_bf, extended)


def spread(value, axes):
    return exchange(jnp.broadcast_to(value[None], (lax.axis_size(axes),) + value.shape), axes)


def swap(value):
    return lax.ppermute(value, C, [(0, 1), (1, 0)])


def body(tokens, proj_weight, cotangent, filters):
    nz = lax.axis_size(ZH)
    nxy = lax.axis_size((X, Y))
    nzl = lax.axis_size(ZL)
    ndp = nz * nxy
    rows, cols = proj_weight.shape
    own_tokens, depth = tokens.shape

    slab_len = cotangent.shape[0]
    core, chip = lax.axis_index(C), lax.axis_index(ZL)
    direct = [tokens] + [None] * (nzl - 1)
    for steps in (2, 1, 3):
        direct[steps] = from_ahead(tokens, ZL, steps)
    sources = (chip + jnp.arange(nzl)) % nzl
    places = jnp.concatenate([2 * sources + core, 2 * sources + 1 - core]).astype(jnp.int32)

    zh, xy = lax.axis_index(ZH), lax.axis_index((X, Y))
    head = cotangent[:8]
    column = spread(jnp.concatenate([proj_weight, head], 0), ZH)
    ahead = lax.dynamic_index_in_dim(column, (zh + 1) % nz, 0, keepdims=False)[rows:]
    column = column[:, :rows].reshape(nz * rows, cols)
    gathered = spread(jnp.concatenate([column, head, ahead], 0), (X, Y))
    heads = lax.dynamic_index_in_dim(gathered, (xy + 1) % nxy, 0, keepdims=False)[nz * rows :]
    following = jnp.where(xy == nxy - 1, heads[8:], heads[:8])
    following = jnp.where(zh * nxy + xy == ndp - 1, jnp.zeros((), BF), following)
    extended = jnp.concatenate([cotangent, following], 0).astype(F32)
    grad_feat = jnp.zeros((slab_len, cols), F32)
    for tap in range(TAPS):
        grad_feat = grad_feat + filters[tap] * extended[tap : tap + slab_len]
    grad_bf = grad_feat.astype(BF)

    chunks = direct + [swap(value) for value in direct]
    slab = in_order(places, chunks)
    packed = local_products(slab, gathered, grad_bf, extended, nz, rows)
    packed, grad_late, gathered = lax.optimization_barrier((packed, grad_bf, gathered))
    total = jnp.sum(exchange(packed, (X, Y)).astype(F32), axis=0)

    weight = gathered[:, : nz * rows].reshape(nxy, nz, rows, cols)
    weight = weight.transpose(1, 0, 2, 3).reshape(depth, cols)
    by_core = grad_late.reshape(nzl, 2, own_tokens, cols)
    theirs = lax.dynamic_index_in_dim(by_core, 1 - core, 1, keepdims=False).reshape(-1, cols)
    ours = lax.dynamic_index_in_dim(by_core, core, 1, keepdims=False).reshape(-1, cols)
    contract_cols = (((1,), (1,)), ((), ()))
    for_other = lax.dot_general(theirs, weight, contract_cols, preferred_element_type=F32).astype(BF)
    from_other = swap(for_other)
    here = lax.dot_general(ours, weight, contract_cols, preferred_element_type=F32)
    chip_sum = (here + from_other.astype(F32)).astype(BF)
    chip_sum = chip_sum.reshape(nzl, own_tokens, depth)
    summed = lax.dynamic_index_in_dim(chip_sum, chip, 0, keepdims=False).astype(F32)
    for steps in (2, 1, 3):
        outgoing = lax.dynamic_index_in_dim(chip_sum, (chip - steps) % nzl, 0, keepdims=False)
        summed = summed + from_ahead(outgoing, ZL, steps).astype(F32)
    input_grad = summed.astype(BF)

    blocks = total[: nz * rows].astype(BF).reshape(nz, rows, cols)
    tail = split_rows(joined_rows(total[nz * rows :]))
    packed = jnp.concatenate([blocks, jnp.broadcast_to(tail[None], (nz, 16, cols))], 1)
    arrived = exchange(packed, ZH)
    arrived, input_grad = lax.optimization_barrier((arrived, input_grad))
    total = jnp.sum(arrived.astype(F32), axis=0)
    weight_grad = total[:rows].astype(BF)
    filter_grad = joined_rows(total[rows:])[:TAPS]
    return input_grad, weight_grad, filter_grad


def solution(mesh):
    fine = Mesh(mesh.devices.reshape(4, 4, 4, 4, 2), (ZH, X, Y, ZL, C))
    dp, seq = (ZH, X, Y), (ZL, C)
    in_specs = (P(dp + seq, None), P(dp, seq), P(dp, seq), P(None, seq))
    out_specs = (P(dp + seq, None), P(dp, seq), P(None, seq))
    return jax.shard_map(body, mesh=fine, in_specs=in_specs, out_specs=out_specs, check_vma=False)
```

```python
import jax
import jax.numpy as jnp
from jax import lax
from jax.experimental import pallas as pl
from jax.experimental.pallas import tpu as pltpu
from jax.sharding import Mesh, PartitionSpec as P

TAPS = 7
VMEM_BYTES = 12 * 1024 * 1024
PRODUCTS_VMEM = 49 * 1024 * 1024
BF = jnp.bfloat16
F32 = jnp.float32
ZH, X, Y, ZL, C = "zh", "x", "y", "zl", "c"


def split_rows(value):
    high = value.astype(BF)
    return jnp.concatenate([high, (value - high.astype(F32)).astype(BF)], 0)


def joined_rows(value):
    half = value.shape[0] // 2
    return value[:half] + value[half:]


def exchange(value, axes):
    return lax.all_to_all(value, axes, split_axis=0, concat_axis=0, tiled=True)


def from_ahead(value, axis, steps):
    count = lax.axis_size(axis)
    return lax.ppermute(value, axis, [(source, (source - steps) % count) for source in range(count)])


def order_kernel(place_ref, *refs):
    chunks, slab_ref = refs[:-1], refs[-1]
    count = chunks[0].shape[0]
    for index, chunk in enumerate(chunks):
        slab_ref[pl.ds(pl.multiple_of(place_ref[index] * count, count), count), :] = chunk[...]


def in_order(places, chunks):
    count, depth = chunks[0].shape
    part = depth // 4
    return pl.pallas_call(
        order_kernel,
        grid_spec=pltpu.PrefetchScalarGridSpec(
            num_scalar_prefetch=1,
            grid=(depth // part,),
            in_specs=[pl.BlockSpec((count, part), lambda i, _: (0, i)) for _ in chunks],
            out_specs=pl.BlockSpec((len(chunks) * count, part), lambda i, _: (0, i)),
        ),
        out_shape=jax.ShapeDtypeStruct((len(chunks) * count, depth), BF),
        compiler_params=pltpu.CompilerParams(vmem_limit_bytes=VMEM_BYTES),
        cost_estimate=pl.CostEstimate(
            flops=8 * 10**9, bytes_accessed=4 * len(chunks) * count * depth, transcendentals=0
        ),
    )(places, *chunks)


def products_kernel(
    core_ref, slab_ref, weight_ref, cotangent_ref, following_ref, filters_ref,
    packed_ref, theirs_out, ours_out, extended_ref, grad_ref, theirs_ref, ours_ref, featured_ref,
):
    step, core = pl.program_id(0), core_ref[0]
    slab_len, cols = grad_ref.shape
    nxy, rows, _ = weight_ref.shape
    half = theirs_ref.shape[0]
    own = slab_len // 8

    @pl.when(step == 0)
    def _():
        extended_ref[:slab_len, :] = cotangent_ref[...].astype(F32)
        extended_ref[slab_len:, :] = following_ref[...]
        grad_feat = filters_ref[0:1, :] * extended_ref[0:slab_len, :]
        for tap in range(1, TAPS):
            grad_feat = grad_feat + filters_ref[tap : tap + 1, :] * extended_ref[tap : tap + slab_len, :]
        grad_ref[...] = grad_feat.astype(BF)
        for index in range(half // own):
            there = pl.ds(pl.multiple_of((2 * index + 1 - core) * own, own), own)
            here = pl.ds(pl.multiple_of((2 * index + core) * own, own), own)
            theirs_ref[index * own : (index + 1) * own, :] = grad_ref[there, :]
            ours_ref[index * own : (index + 1) * own, :] = grad_ref[here, :]

    weight = weight_ref[...].reshape(nxy * rows, cols)
    contract_cols = (((1,), (1,)), ((), ()))
    theirs_out[...] = lax.dot_general(
        theirs_ref[...], weight, contract_cols, preferred_element_type=F32
    ).astype(BF)
    ours_out[...] = lax.dot_general(
        ours_ref[...], weight, contract_cols, preferred_element_type=F32
    ).astype(BF)
    products = lax.dot_general(
        slab_ref[...], grad_ref[...], (((0,), (0,)), ((), ())), preferred_element_type=F32
    )
    place = pl.ds(pl.multiple_of(step * rows, rows), rows)
    packed_ref[:, place, :] = products.astype(BF).reshape(nxy, rows, cols)
    term = jnp.dot(slab_ref[...], weight, preferred_element_type=F32)

    @pl.when(step == 0)
    def _():
        featured_ref[...] = term

    @pl.when(step > 0)
    def _():
        featured_ref[...] += term

    @pl.when(step == pl.num_programs(0) - 1)
    def _():
        featured = featured_ref[...].astype(BF).astype(F32)
        sums = [
            jnp.sum(featured * extended_ref[tap : tap + slab_len, :], axis=0, keepdims=True)
            for tap in range(TAPS)
        ]
        tail = split_rows(jnp.concatenate(sums + [jnp.zeros((1, cols), F32)], 0))
        packed_ref[:, pl.num_programs(0) * rows :, :] = jnp.broadcast_to(tail[None], (nxy, 16, cols))


def local_products(core, slab, gathered, cotangent, following, filters, nz, rows):
    slab_len, depth = slab.shape
    nxy, _, cols = gathered.shape
    part = nxy * rows
    half = slab_len // 2
    return pl.pallas_call(
        products_kernel,
        grid_spec=pltpu.PrefetchScalarGridSpec(
            num_scalar_prefetch=1,
            grid=(nz,),
            in_specs=[
                pl.BlockSpec((slab_len, part), lambda i, _: (0, i)),
                pl.BlockSpec((nxy, rows, cols), lambda i, _: (0, i, 0)),
                pl.BlockSpec((slab_len, cols), lambda i, _: (0, 0)),
                pl.BlockSpec(following.shape, lambda i, _: (0, 0)),
                pl.BlockSpec(filters.shape, lambda i, _: (0, 0)),
            ],
            out_specs=[
                pl.BlockSpec((nxy, nz * rows + 16, cols), lambda i, _: (0, 0, 0)),
                pl.BlockSpec((half, part), lambda i, _: (0, i)),
                pl.BlockSpec((half, part), lambda i, _: (0, i)),
            ],
            scratch_shapes=[
                pltpu.VMEM((slab_len + 8, cols), F32),
                pltpu.VMEM((slab_len, cols), BF),
                pltpu.VMEM((half, cols), BF),
                pltpu.VMEM((half, cols), BF),
                pltpu.VMEM((slab_len, cols), F32),
            ],
        ),
        out_shape=[
            jax.ShapeDtypeStruct((nxy, nz * rows + 16, cols), BF),
            jax.ShapeDtypeStruct((half, depth), BF),
            jax.ShapeDtypeStruct((half, depth), BF),
        ],
        compiler_params=pltpu.CompilerParams(vmem_limit_bytes=PRODUCTS_VMEM),
        cost_estimate=pl.CostEstimate(
            flops=6 * slab_len * depth * cols, bytes_accessed=6 * slab_len * depth, transcendentals=0
        ),
    )(core.reshape(1).astype(jnp.int32), slab, gathered, cotangent, following, filters)


def spread(value, axes):
    return exchange(jnp.broadcast_to(value[None], (lax.axis_size(axes),) + value.shape), axes)


def swap(value):
    return lax.ppermute(value, C, [(0, 1), (1, 0)])


def body(tokens, proj_weight, cotangent, filters):
    nz = lax.axis_size(ZH)
    nxy = lax.axis_size((X, Y))
    nzl = lax.axis_size(ZL)
    ndp = nz * nxy
    rows, cols = proj_weight.shape
    own_tokens, depth = tokens.shape

    slab_len = cotangent.shape[0]
    core, chip = lax.axis_index(C), lax.axis_index(ZL)
    direct = [tokens] + [None] * (nzl - 1)
    for steps in (2, 1, 3):
        direct[steps] = from_ahead(tokens, ZL, steps)
    sources = (chip + jnp.arange(nzl)) % nzl
    places = jnp.concatenate([2 * sources + core, 2 * sources + 1 - core]).astype(jnp.int32)

    zh, xy = lax.axis_index(ZH), lax.axis_index((X, Y))
    head = cotangent[:8]
    column = spread(jnp.concatenate([proj_weight, head], 0), ZH)
    ahead = lax.dynamic_index_in_dim(column, (zh + 1) % nz, 0, keepdims=False)[rows:]
    column = column[:, :rows].reshape(nz * rows, cols)
    gathered = spread(jnp.concatenate([column, head, ahead], 0), (X, Y))
    heads = lax.dynamic_index_in_dim(gathered, (xy + 1) % nxy, 0, keepdims=False)[nz * rows :]
    following = jnp.where(xy == nxy - 1, heads[8:], heads[:8])
    following = jnp.where(zh * nxy + xy == ndp - 1, jnp.zeros((), BF), following).astype(F32)
    chunks = direct + [swap(value) for value in direct]
    slab = in_order(places, chunks)
    packed, for_other, here = local_products(
        core, slab, gathered, cotangent, following, filters, nz, rows
    )
    total = jnp.sum(exchange(packed, (X, Y)).astype(F32), axis=0)

    chip_sum = (here.astype(F32) + swap(for_other).astype(F32)).astype(BF)
    chip_sum = chip_sum.reshape(nzl, own_tokens, depth)
    summed = lax.dynamic_index_in_dim(chip_sum, chip, 0, keepdims=False).astype(F32)
    for steps in (2, 1, 3):
        outgoing = lax.dynamic_index_in_dim(chip_sum, (chip - steps) % nzl, 0, keepdims=False)
        summed = summed + from_ahead(outgoing, ZL, steps).astype(F32)
    input_grad = summed.astype(BF)

    blocks = total[: nz * rows].astype(BF).reshape(nz, rows, cols)
    tail = split_rows(joined_rows(total[nz * rows :]))
    packed = jnp.concatenate([blocks, jnp.broadcast_to(tail[None], (nz, 16, cols))], 1)
    arrived = exchange(packed, ZH)
    arrived, input_grad = lax.optimization_barrier((arrived, input_grad))
    total = jnp.sum(arrived.astype(F32), axis=0)
    weight_grad = total[:rows].astype(BF)
    filter_grad = joined_rows(total[rows:])[:TAPS]
    return input_grad, weight_grad, filter_grad


def solution(mesh):
    fine = Mesh(mesh.devices.reshape(4, 4, 4, 4, 2), (ZH, X, Y, ZL, C))
    dp, seq = (ZH, X, Y), (ZL, C)
    in_specs = (P(dp + seq, None), P(dp, seq), P(dp, seq), P(None, seq))
    out_specs = (P(dp + seq, None), P(dp, seq), P(None, seq))
    return jax.shard_map(body, mesh=fine, in_specs=in_specs, out_specs=out_specs, check_vma=False)
```

```python
import jax
import jax.numpy as jnp
from jax import lax
from jax.experimental import pallas as pl
from jax.experimental.pallas import tpu as pltpu
from jax.sharding import Mesh, PartitionSpec as P

TAPS = 7
VMEM_BYTES = 12 * 1024 * 1024
PRODUCTS_VMEM = 49 * 1024 * 1024
BF = jnp.bfloat16
F32 = jnp.float32
ZH, X, Y, ZL, C = "zh", "x", "y", "zl", "c"


def split_rows(value):
    high = value.astype(BF)
    return jnp.concatenate([high, (value - high.astype(F32)).astype(BF)], 0)


def joined_rows(value):
    half = value.shape[0] // 2
    return value[:half] + value[half:]


def exchange(value, axes):
    return lax.all_to_all(value, axes, split_axis=0, concat_axis=0, tiled=True)


def from_ahead(value, axis, steps):
    count = lax.axis_size(axis)
    return lax.ppermute(value, axis, [(source, (source - steps) % count) for source in range(count)])


def order_kernel(place_ref, *refs):
    chunks, slab_ref = refs[:-1], refs[-1]
    count = chunks[0].shape[0]
    for index, chunk in enumerate(chunks):
        slab_ref[pl.ds(pl.multiple_of(place_ref[index] * count, count), count), :] = chunk[...]


def in_order(places, chunks):
    count, depth = chunks[0].shape
    part = depth // 4
    return pl.pallas_call(
        order_kernel,
        grid_spec=pltpu.PrefetchScalarGridSpec(
            num_scalar_prefetch=1,
            grid=(depth // part,),
            in_specs=[pl.BlockSpec((count, part), lambda i, _: (0, i)) for _ in chunks],
            out_specs=pl.BlockSpec((len(chunks) * count, part), lambda i, _: (0, i)),
        ),
        out_shape=jax.ShapeDtypeStruct((len(chunks) * count, depth), BF),
        compiler_params=pltpu.CompilerParams(vmem_limit_bytes=VMEM_BYTES),
        cost_estimate=pl.CostEstimate(
            flops=4 * 10**9, bytes_accessed=4 * len(chunks) * count * depth, transcendentals=0
        ),
    )(places, *chunks)


def products_kernel(
    core_ref, slab_ref, weight_ref, cotangent_ref, early_ref, following_ref, filters_ref,
    packed_ref, theirs_out, ours_out, extended_ref, grad_ref, theirs_ref, ours_ref, featured_ref,
):
    step, core = pl.program_id(0), core_ref[0]
    slab_len, cols = grad_ref.shape
    nxy, rows, _ = weight_ref.shape
    half = theirs_ref.shape[0]
    own = slab_len // 8

    @pl.when(step == 0)
    def _():
        extended_ref[:slab_len, :] = cotangent_ref[...].astype(F32)
        extended_ref[slab_len:, :] = following_ref[...]
        last = slab_len - 16
        grad_feat = filters_ref[0:1, :] * extended_ref[last:slab_len, :]
        for tap in range(1, TAPS):
            grad_feat = grad_feat + filters_ref[tap : tap + 1, :] * extended_ref[last + tap : slab_len + tap, :]
        grad_ref[:last, :] = early_ref[:last, :]
        grad_ref[last:, :] = grad_feat.astype(BF)
        for index in range(half // own):
            there = pl.ds(pl.multiple_of((2 * index + 1 - core) * own, own), own)
            here = pl.ds(pl.multiple_of((2 * index + core) * own, own), own)
            theirs_ref[index * own : (index + 1) * own, :] = grad_ref[there, :]
            ours_ref[index * own : (index + 1) * own, :] = grad_ref[here, :]

    weight = weight_ref[...].reshape(nxy * rows, cols)
    contract_cols = (((1,), (1,)), ((), ()))
    theirs_out[...] = lax.dot_general(
        theirs_ref[...], weight, contract_cols, preferred_element_type=F32
    ).astype(BF)
    ours_out[...] = lax.dot_general(
        ours_ref[...], weight, contract_cols, preferred_element_type=F32
    ).astype(BF)
    products = lax.dot_general(
        slab_ref[...], grad_ref[...], (((0,), (0,)), ((), ())), preferred_element_type=F32
    )
    place = pl.ds(pl.multiple_of(step * rows, rows), rows)
    packed_ref[:, place, :] = products.astype(BF).reshape(nxy, rows, cols)
    term = jnp.dot(slab_ref[...], weight, preferred_element_type=F32)

    @pl.when(step == 0)
    def _():
        featured_ref[...] = term

    @pl.when(step > 0)
    def _():
        featured_ref[...] += term

    @pl.when(step == pl.num_programs(0) - 1)
    def _():
        featured = featured_ref[...].astype(BF).astype(F32)
        sums = [
            jnp.sum(featured * extended_ref[tap : tap + slab_len, :], axis=0, keepdims=True)
            for tap in range(TAPS)
        ]
        tail = split_rows(jnp.concatenate(sums + [jnp.zeros((1, cols), F32)], 0))
        packed_ref[:, pl.num_programs(0) * rows :, :] = jnp.broadcast_to(tail[None], (nxy, 16, cols))


def local_products(core, slab, gathered, cotangent, early, following, filters, nz, rows):
    slab_len, depth = slab.shape
    nxy, _, cols = gathered.shape
    part = nxy * rows
    half = slab_len // 2
    return pl.pallas_call(
        products_kernel,
        grid_spec=pltpu.PrefetchScalarGridSpec(
            num_scalar_prefetch=1,
            grid=(nz,),
            in_specs=[
                pl.BlockSpec((slab_len, part), lambda i, _: (0, i)),
                pl.BlockSpec((nxy, rows, cols), lambda i, _: (0, i, 0)),
                pl.BlockSpec((slab_len, cols), lambda i, _: (0, 0)),
                pl.BlockSpec((slab_len, cols), lambda i, _: (0, 0)),
                pl.BlockSpec(following.shape, lambda i, _: (0, 0)),
                pl.BlockSpec(filters.shape, lambda i, _: (0, 0)),
            ],
            out_specs=[
                pl.BlockSpec((nxy, nz * rows + 16, cols), lambda i, _: (0, 0, 0)),
                pl.BlockSpec((half, part), lambda i, _: (0, i)),
                pl.BlockSpec((half, part), lambda i, _: (0, i)),
            ],
            scratch_shapes=[
                pltpu.VMEM((slab_len + 8, cols), F32),
                pltpu.VMEM((slab_len, cols), BF),
                pltpu.VMEM((half, cols), BF),
                pltpu.VMEM((half, cols), BF),
                pltpu.VMEM((slab_len, cols), F32),
            ],
        ),
        out_shape=[
            jax.ShapeDtypeStruct((nxy, nz * rows + 16, cols), BF),
            jax.ShapeDtypeStruct((half, depth), BF),
            jax.ShapeDtypeStruct((half, depth), BF),
        ],
        compiler_params=pltpu.CompilerParams(vmem_limit_bytes=PRODUCTS_VMEM),
        cost_estimate=pl.CostEstimate(
            flops=6 * slab_len * depth * cols, bytes_accessed=6 * slab_len * depth, transcendentals=0
        ),
    )(core.reshape(1).astype(jnp.int32), slab, gathered, cotangent, early, following, filters)


def spread(value, axes):
    return exchange(jnp.broadcast_to(value[None], (lax.axis_size(axes),) + value.shape), axes)


def swap(value):
    return lax.ppermute(value, C, [(0, 1), (1, 0)])


def body(tokens, proj_weight, cotangent, filters):
    nz = lax.axis_size(ZH)
    nxy = lax.axis_size((X, Y))
    nzl = lax.axis_size(ZL)
    ndp = nz * nxy
    rows, cols = proj_weight.shape
    own_tokens, depth = tokens.shape

    slab_len = cotangent.shape[0]
    core, chip = lax.axis_index(C), lax.axis_index(ZL)
    direct = [tokens] + [None] * (nzl - 1)
    for steps in (2, 1, 3):
        direct[steps] = from_ahead(tokens, ZL, steps)
    sources = (chip + jnp.arange(nzl)) % nzl
    places = jnp.concatenate([2 * sources + core, 2 * sources + 1 - core]).astype(jnp.int32)

    extended = jnp.pad(cotangent, ((0, 8), (0, 0))).astype(F32)
    early = filters[0] * extended[:slab_len]
    for tap in range(1, TAPS):
        early = early + filters[tap] * extended[tap : tap + slab_len]
    early = early.astype(BF)

    zh, xy = lax.axis_index(ZH), lax.axis_index((X, Y))
    head = cotangent[:8]
    column = spread(jnp.concatenate([proj_weight, head], 0), ZH)
    ahead = lax.dynamic_index_in_dim(column, (zh + 1) % nz, 0, keepdims=False)[rows:]
    column = column[:, :rows].reshape(nz * rows, cols)
    gathered = spread(jnp.concatenate([column, head, ahead], 0), (X, Y))
    heads = lax.dynamic_index_in_dim(gathered, (xy + 1) % nxy, 0, keepdims=False)[nz * rows :]
    following = jnp.where(xy == nxy - 1, heads[8:], heads[:8])
    following = jnp.where(zh * nxy + xy == ndp - 1, jnp.zeros((), BF), following).astype(F32)
    chunks = direct + [swap(value) for value in direct]
    slab = in_order(places, chunks)
    packed, for_other, here = local_products(
        core, slab, gathered, cotangent, early, following, filters, nz, rows
    )
    total = jnp.sum(exchange(packed, (X, Y)).astype(F32), axis=0)

    chip_sum = (here.astype(F32) + swap(for_other).astype(F32)).astype(BF)
    chip_sum = chip_sum.reshape(nzl, own_tokens, depth)
    summed = lax.dynamic_index_in_dim(chip_sum, chip, 0, keepdims=False).astype(F32)
    for steps in (2, 1, 3):
        outgoing = lax.dynamic_index_in_dim(chip_sum, (chip - steps) % nzl, 0, keepdims=False)
        summed = summed + from_ahead(outgoing, ZL, steps).astype(F32)
    input_grad = summed.astype(BF)

    blocks = total[: nz * rows].astype(BF).reshape(nz, rows, cols)
    tail = split_rows(joined_rows(total[nz * rows :]))
    packed = jnp.concatenate([blocks, jnp.broadcast_to(tail[None], (nz, 16, cols))], 1)
    arrived = exchange(packed, ZH)
    arrived, input_grad = lax.optimization_barrier((arrived, input_grad))
    total = jnp.sum(arrived.astype(F32), axis=0)
    weight_grad = total[:rows].astype(BF)
    filter_grad = joined_rows(total[rows:])[:TAPS]
    return input_grad, weight_grad, filter_grad


def solution(mesh):
    fine = Mesh(mesh.devices.reshape(4, 4, 4, 4, 2), (ZH, X, Y, ZL, C))
    dp, seq = (ZH, X, Y), (ZL, C)
    in_specs = (P(dp + seq, None), P(dp, seq), P(dp, seq), P(None, seq))
    out_specs = (P(dp + seq, None), P(dp, seq), P(None, seq))
    return jax.shard_map(body, mesh=fine, in_specs=in_specs, out_specs=out_specs, check_vma=False)
```

```python
import jax
import jax.numpy as jnp
from jax import lax
from jax.experimental import pallas as pl
from jax.experimental.pallas import tpu as pltpu
from jax.sharding import Mesh, PartitionSpec as P

TAPS = 7
VMEM_BYTES = 12 * 1024 * 1024
PRODUCTS_VMEM = 49 * 1024 * 1024
BF = jnp.bfloat16
F32 = jnp.float32
ZH, X, Y, ZL, C = "zh", "x", "y", "zl", "c"


def split_rows(value):
    high = value.astype(BF)
    return jnp.concatenate([high, (value - high.astype(F32)).astype(BF)], 0)


def joined_rows(value):
    half = value.shape[0] // 2
    return value[:half] + value[half:]


def exchange(value, axes):
    return lax.all_to_all(value, axes, split_axis=0, concat_axis=0, tiled=True)


def from_ahead(value, axis, steps):
    count = lax.axis_size(axis)
    return lax.ppermute(value, axis, [(source, (source - steps) % count) for source in range(count)])


def order_kernel(*refs):
    chunks, (slab_ref, done) = refs[:-2], refs[-2:]
    count, chips = chunks[0].shape[0], len(chunks) // 2
    core, chip = lax.axis_index(C), lax.axis_index(ZL)
    copies = []
    for index, chunk in enumerate(chunks):
        source = lax.rem(chip + index % chips, chips)
        place = 2 * source + (core if index < chips else 1 - core)
        rows = pl.ds(pl.multiple_of(place * count, count), count)
        copies.append(pltpu.make_async_copy(chunk, slab_ref.at[rows, :], done.at[index]))
        copies[-1].start()
    for copy in copies:
        copy.wait()


def in_order(chunks):
    count, depth = chunks[0].shape
    return pl.pallas_call(
        order_kernel,
        in_specs=[pl.BlockSpec(memory_space=pl.ANY) for _ in chunks],
        out_specs=pl.BlockSpec(memory_space=pltpu.HBM),
        out_shape=pltpu.HBM((len(chunks) * count, depth), BF),
        scratch_shapes=[pltpu.SemaphoreType.DMA((len(chunks),))],
        compiler_params=pltpu.CompilerParams(vmem_limit_bytes=VMEM_BYTES),
        cost_estimate=pl.CostEstimate(
            flops=8 * 10**9, bytes_accessed=4 * len(chunks) * count * depth, transcendentals=0
        ),
    )(*chunks)


def products_kernel(
    core_ref, slab_ref, weight_ref, cotangent_ref, following_ref, filters_ref,
    packed_ref, theirs_out, ours_out, extended_ref, grad_ref, theirs_ref, featured_ref,
):
    step, core = pl.program_id(0), core_ref[0]
    slab_len, cols = grad_ref.shape
    nxy, rows, _ = weight_ref.shape
    half = theirs_ref.shape[0]
    own = slab_len // 8

    @pl.when(step == 0)
    def _():
        extended_ref[:slab_len, :] = cotangent_ref[...].astype(F32)
        extended_ref[slab_len:, :] = following_ref[...]
        grad_feat = filters_ref[0:1, :] * extended_ref[0:slab_len, :]
        for tap in range(1, TAPS):
            grad_feat = grad_feat + filters_ref[tap : tap + 1, :] * extended_ref[tap : tap + slab_len, :]
        grad_ref[...] = grad_feat.astype(BF)
        for index in range(half // own):
            there = pl.ds(pl.multiple_of((2 * index + 1 - core) * own, own), own)
            here = pl.ds(pl.multiple_of((2 * index + core) * own, own), own)
            theirs_ref[index * own : (index + 1) * own, :] = grad_ref[there, :]
            ours_out[index * own : (index + 1) * own, :] = grad_ref[here, :]

    weight = weight_ref[...].reshape(nxy * rows, cols)
    contract_cols = (((1,), (1,)), ((), ()))
    theirs_out[...] = lax.dot_general(
        theirs_ref[...], weight, contract_cols, preferred_element_type=F32
    ).astype(BF)
    products = lax.dot_general(
        slab_ref[...], grad_ref[...], (((0,), (0,)), ((), ())), preferred_element_type=F32
    )
    place = pl.ds(pl.multiple_of(step * rows, rows), rows)
    packed_ref[:, place, :] = products.astype(BF).reshape(nxy, rows, cols)
    term = jnp.dot(slab_ref[...], weight, preferred_element_type=F32)

    @pl.when(step == 0)
    def _():
        featured_ref[...] = term

    @pl.when(step > 0)
    def _():
        featured_ref[...] += term

    @pl.when(step == pl.num_programs(0) - 1)
    def _():
        featured = featured_ref[...].astype(BF).astype(F32)
        sums = [
            jnp.sum(featured * extended_ref[tap : tap + slab_len, :], axis=0, keepdims=True)
            for tap in range(TAPS)
        ]
        tail = split_rows(jnp.concatenate(sums + [jnp.zeros((1, cols), F32)], 0))
        packed_ref[:, pl.num_programs(0) * rows :, :] = jnp.broadcast_to(tail[None], (nxy, 16, cols))


def local_products(core, slab, gathered, cotangent, following, filters, nz, rows):
    slab_len, depth = slab.shape
    nxy, _, cols = gathered.shape
    part = nxy * rows
    half = slab_len // 2
    return pl.pallas_call(
        products_kernel,
        grid_spec=pltpu.PrefetchScalarGridSpec(
            num_scalar_prefetch=1,
            grid=(nz,),
            in_specs=[
                pl.BlockSpec((slab_len, part), lambda i, _: (0, i)),
                pl.BlockSpec((nxy, rows, cols), lambda i, _: (0, i, 0)),
                pl.BlockSpec((slab_len, cols), lambda i, _: (0, 0)),
                pl.BlockSpec(following.shape, lambda i, _: (0, 0)),
                pl.BlockSpec(filters.shape, lambda i, _: (0, 0)),
            ],
            out_specs=[
                pl.BlockSpec((nxy, nz * rows + 16, cols), lambda i, _: (0, 0, 0)),
                pl.BlockSpec((half, part), lambda i, _: (0, i)),
                pl.BlockSpec((half, cols), lambda i, _: (0, 0)),
            ],
            scratch_shapes=[
                pltpu.VMEM((slab_len + 8, cols), F32),
                pltpu.VMEM((slab_len, cols), BF),
                pltpu.VMEM((half, cols), BF),
                pltpu.VMEM((slab_len, cols), F32),
            ],
        ),
        out_shape=[
            jax.ShapeDtypeStruct((nxy, nz * rows + 16, cols), BF),
            jax.ShapeDtypeStruct((half, depth), BF),
            jax.ShapeDtypeStruct((half, cols), BF),
        ],
        compiler_params=pltpu.CompilerParams(vmem_limit_bytes=PRODUCTS_VMEM),
        cost_estimate=pl.CostEstimate(
            flops=6 * slab_len * depth * cols, bytes_accessed=6 * slab_len * depth, transcendentals=0
        ),
    )(core.reshape(1).astype(jnp.int32), slab, gathered, cotangent, following, filters)


def own_kernel(ours_ref, weight_ref, out_ref):
    weight = weight_ref[...].reshape(-1, ours_ref.shape[1])
    out_ref[...] = lax.dot_general(
        ours_ref[...], weight, (((1,), (1,)), ((), ())), preferred_element_type=F32
    ).astype(BF)


def own_products(ours, gathered, nz, rows):
    half, cols = ours.shape
    nxy = gathered.shape[0]
    part = nxy * rows
    return pl.pallas_call(
        own_kernel,
        grid=(nz,),
        in_specs=[
            pl.BlockSpec((half, cols), lambda i: (0, 0)),
            pl.BlockSpec((nxy, rows, cols), lambda i: (0, i, 0)),
        ],
        out_specs=pl.BlockSpec((half, part), lambda i: (0, i)),
        out_shape=jax.ShapeDtypeStruct((half, nz * part), BF),
        compiler_params=pltpu.CompilerParams(vmem_limit_bytes=VMEM_BYTES),
        cost_estimate=pl.CostEstimate(flops=4 * 10**9, bytes_accessed=8 * half * part, transcendentals=0),
    )(ours, gathered)


def head_kernel(weight_ref, head_ref, out_ref):
    rows = weight_ref.shape[0]
    for index in range(out_ref.shape[0]):
        out_ref[index, :rows, :] = weight_ref[...]
        out_ref[index, rows:, :] = head_ref[...]


def with_head(proj_weight, cotangent, nz):
    rows, cols = proj_weight.shape
    return pl.pallas_call(
        head_kernel,
        grid=(1,),
        in_specs=[
            pl.BlockSpec((rows, cols), lambda i: (0, 0)),
            pl.BlockSpec((16, cols), lambda i: (0, 0)),
        ],
        out_specs=pl.BlockSpec((nz, rows + 16, cols), lambda i: (0, 0, 0)),
        out_shape=jax.ShapeDtypeStruct((nz, rows + 16, cols), BF),
        compiler_params=pltpu.CompilerParams(vmem_limit_bytes=60 * 1024 * 1024),
    )(proj_weight, cotangent)


def spread(value, axes):
    return exchange(jnp.broadcast_to(value[None], (lax.axis_size(axes),) + value.shape), axes)


def swap(value):
    return lax.ppermute(value, C, [(0, 1), (1, 0)])


def body(tokens, proj_weight, cotangent, filters):
    nz = lax.axis_size(ZH)
    nxy = lax.axis_size((X, Y))
    nzl = lax.axis_size(ZL)
    ndp = nz * nxy
    rows, cols = proj_weight.shape
    own_tokens, depth = tokens.shape

    slab_len = cotangent.shape[0]
    core, chip = lax.axis_index(C), lax.axis_index(ZL)
    direct = [tokens] + [None] * (nzl - 1)
    for steps in (2, 1, 3):
        direct[steps] = from_ahead(tokens, ZL, steps)

    zh, xy = lax.axis_index(ZH), lax.axis_index((X, Y))
    head = cotangent[:8]
    column = exchange(with_head(proj_weight, cotangent, nz), ZH)
    ahead = lax.dynamic_index_in_dim(column, (zh + 1) % nz, 0, keepdims=False)[rows : rows + 8]
    column = column[:, :rows].reshape(nz * rows, cols)
    gathered = spread(jnp.concatenate([column, head, ahead], 0), (X, Y))
    heads = lax.dynamic_index_in_dim(gathered, (xy + 1) % nxy, 0, keepdims=False)[nz * rows :]
    following = jnp.where(xy == nxy - 1, heads[8:], heads[:8])
    following = jnp.where(zh * nxy + xy == ndp - 1, jnp.zeros((), BF), following).astype(F32)
    chunks = direct + [swap(value) for value in direct]
    slab = in_order(chunks)
    packed, for_other, ours = local_products(
        core, slab, gathered, cotangent, following, filters, nz, rows
    )
    total = jnp.sum(exchange(packed, (X, Y)).astype(F32), axis=0)

    here = own_products(ours, gathered, nz, rows)
    chip_sum = (here.astype(F32) + swap(for_other).astype(F32)).astype(BF)
    chip_sum = chip_sum.reshape(nzl, own_tokens, depth)
    summed = lax.dynamic_index_in_dim(chip_sum, chip, 0, keepdims=False).astype(F32)
    for steps in (2, 1, 3):
        outgoing = lax.dynamic_index_in_dim(chip_sum, (chip - steps) % nzl, 0, keepdims=False)
        summed = summed + from_ahead(outgoing, ZL, steps).astype(F32)
    input_grad = summed.astype(BF)

    blocks = total[: nz * rows].astype(BF).reshape(nz, rows, cols)
    tail = split_rows(joined_rows(total[nz * rows :]))
    packed = jnp.concatenate([blocks, jnp.broadcast_to(tail[None], (nz, 16, cols))], 1)
    arrived = exchange(packed, ZH)
    arrived, input_grad = lax.optimization_barrier((arrived, input_grad))
    total = jnp.sum(arrived.astype(F32), axis=0)
    weight_grad = total[:rows].astype(BF)
    filter_grad = joined_rows(total[rows:])[:TAPS]
    return input_grad, weight_grad, filter_grad


def solution(mesh):
    fine = Mesh(mesh.devices.reshape(4, 4, 4, 4, 2), (ZH, X, Y, ZL, C))
    dp, seq = (ZH, X, Y), (ZL, C)
    in_specs = (P(dp + seq, None), P(dp, seq), P(dp, seq), P(None, seq))
    out_specs = (P(dp + seq, None), P(dp, seq), P(None, seq))
    return jax.shard_map(body, mesh=fine, in_specs=in_specs, out_specs=out_specs, check_vma=False)
```

```python
import jax
import jax.numpy as jnp
from jax import lax
from jax.experimental import pallas as pl
from jax.experimental.pallas import tpu as pltpu
from jax.sharding import Mesh, PartitionSpec as P

TAPS = 7
VMEM_BYTES = 12 * 1024 * 1024
PRODUCTS_VMEM = 49 * 1024 * 1024
BF = jnp.bfloat16
F32 = jnp.float32
ZH, X, Y, ZL, C = "zh", "x", "y", "zl", "c"


def split_rows(value):
    high = value.astype(BF)
    return jnp.concatenate([high, (value - high.astype(F32)).astype(BF)], 0)


def joined_rows(value):
    half = value.shape[0] // 2
    return value[:half] + value[half:]


def exchange(value, axes):
    return lax.all_to_all(value, axes, split_axis=0, concat_axis=0, tiled=True)


def from_ahead(value, axis, steps):
    count = lax.axis_size(axis)
    return lax.ppermute(value, axis, [(source, (source - steps) % count) for source in range(count)])


def order_kernel(*refs):
    chunks, (slab_ref, done) = refs[:-2], refs[-2:]
    count, chips = chunks[0].shape[0], len(chunks) // 2
    core, chip = lax.axis_index(C), lax.axis_index(ZL)
    copies = []
    for index, chunk in enumerate(chunks):
        source = lax.rem(chip + index % chips, chips)
        place = 2 * source + (core if index < chips else 1 - core)
        rows = pl.ds(pl.multiple_of(place * count, count), count)
        copies.append(pltpu.make_async_copy(chunk, slab_ref.at[rows, :], done.at[index]))
        copies[-1].start()
    for copy in copies:
        copy.wait()


def in_order(chunks):
    count, depth = chunks[0].shape
    return pl.pallas_call(
        order_kernel,
        in_specs=[pl.BlockSpec(memory_space=pl.ANY) for _ in chunks],
        out_specs=pl.BlockSpec(memory_space=pltpu.HBM),
        out_shape=pltpu.HBM((len(chunks) * count, depth), BF),
        scratch_shapes=[pltpu.SemaphoreType.DMA((len(chunks),))],
        compiler_params=pltpu.CompilerParams(vmem_limit_bytes=VMEM_BYTES),
        cost_estimate=pl.CostEstimate(
            flops=8 * 10**9, bytes_accessed=4 * len(chunks) * count * depth, transcendentals=0
        ),
    )(*chunks)


def products_kernel(
    core_ref, slab_ref, weight_ref, cotangent_ref, following_ref, filters_ref,
    packed_ref, theirs_out, ours_out, extended_ref, grad_ref, theirs_ref, featured_ref,
):
    step, core = pl.program_id(0), core_ref[0]
    slab_len, cols = grad_ref.shape
    nxy, rows, _ = weight_ref.shape
    half = theirs_ref.shape[0]
    own = slab_len // 8

    @pl.when(step == 0)
    def _():
        extended_ref[:slab_len, :] = cotangent_ref[...].astype(F32)
        extended_ref[slab_len:, :] = following_ref[...]
        grad_feat = filters_ref[0:1, :] * extended_ref[0:slab_len, :]
        for tap in range(1, TAPS):
            grad_feat = grad_feat + filters_ref[tap : tap + 1, :] * extended_ref[tap : tap + slab_len, :]
        grad_ref[...] = grad_feat.astype(BF)
        for index in range(half // own):
            there = pl.ds(pl.multiple_of((2 * index + 1 - core) * own, own), own)
            here = pl.ds(pl.multiple_of((2 * index + core) * own, own), own)
            theirs_ref[index * own : (index + 1) * own, :] = grad_ref[there, :]
            ours_out[index * own : (index + 1) * own, :] = grad_ref[here, :]

    weight = weight_ref[...].reshape(nxy * rows, cols)
    contract_cols = (((1,), (1,)), ((), ()))
    theirs_out[...] = lax.dot_general(
        theirs_ref[...], weight, contract_cols, preferred_element_type=F32
    ).astype(BF)
    products = lax.dot_general(
        slab_ref[...], grad_ref[...], (((0,), (0,)), ((), ())), preferred_element_type=F32
    )
    place = pl.ds(pl.multiple_of(step * rows, rows), rows)
    packed_ref[:, place, :] = products.astype(BF).reshape(nxy, rows, cols)
    term = jnp.dot(slab_ref[...], weight, preferred_element_type=F32)

    @pl.when(step == 0)
    def _():
        featured_ref[...] = term

    @pl.when(step > 0)
    def _():
        featured_ref[...] += term

    @pl.when(step == pl.num_programs(0) - 1)
    def _():
        featured = featured_ref[...].astype(BF).astype(F32)
        sums = [
            jnp.sum(featured * extended_ref[tap : tap + slab_len, :], axis=0, keepdims=True)
            for tap in range(TAPS)
        ]
        tail = split_rows(jnp.concatenate(sums + [jnp.zeros((1, cols), F32)], 0))
        packed_ref[:, pl.num_programs(0) * rows :, :] = jnp.broadcast_to(tail[None], (nxy, 16, cols))


def local_products(core, slab, gathered, cotangent, following, filters, nz, rows):
    slab_len, depth = slab.shape
    nxy, _, cols = gathered.shape
    part = nxy * rows
    half = slab_len // 2
    return pl.pallas_call(
        products_kernel,
        grid_spec=pltpu.PrefetchScalarGridSpec(
            num_scalar_prefetch=1,
            grid=(nz,),
            in_specs=[
                pl.BlockSpec((slab_len, part), lambda i, _: (0, i)),
                pl.BlockSpec((nxy, rows, cols), lambda i, _: (0, i, 0)),
                pl.BlockSpec((slab_len, cols), lambda i, _: (0, 0)),
                pl.BlockSpec(following.shape, lambda i, _: (0, 0)),
                pl.BlockSpec(filters.shape, lambda i, _: (0, 0)),
            ],
            out_specs=[
                pl.BlockSpec((nxy, nz * rows + 16, cols), lambda i, _: (0, 0, 0)),
                pl.BlockSpec((half, part), lambda i, _: (0, i)),
                pl.BlockSpec((half, cols), lambda i, _: (0, 0)),
            ],
            scratch_shapes=[
                pltpu.VMEM((slab_len + 8, cols), F32),
                pltpu.VMEM((slab_len, cols), BF),
                pltpu.VMEM((half, cols), BF),
                pltpu.VMEM((slab_len, cols), F32),
            ],
        ),
        out_shape=[
            jax.ShapeDtypeStruct((nxy, nz * rows + 16, cols), BF),
            jax.ShapeDtypeStruct((half, depth), BF),
            jax.ShapeDtypeStruct((half, cols), BF),
        ],
        compiler_params=pltpu.CompilerParams(vmem_limit_bytes=PRODUCTS_VMEM),
        cost_estimate=pl.CostEstimate(
            flops=6 * slab_len * depth * cols, bytes_accessed=6 * slab_len * depth, transcendentals=0
        ),
    )(core.reshape(1).astype(jnp.int32), slab, gathered, cotangent, following, filters)


def own_kernel(ours_ref, weight_ref, out_ref):
    weight = weight_ref[...].reshape(-1, ours_ref.shape[1])
    out_ref[...] = lax.dot_general(
        ours_ref[...], weight, (((1,), (1,)), ((), ())), preferred_element_type=F32
    ).astype(BF)


def own_products(ours, gathered, nz, rows):
    half, cols = ours.shape
    nxy = gathered.shape[0]
    part = nxy * rows
    return pl.pallas_call(
        own_kernel,
        grid=(nz,),
        in_specs=[
            pl.BlockSpec((half, cols), lambda i: (0, 0)),
            pl.BlockSpec((nxy, rows, cols), lambda i: (0, i, 0)),
        ],
        out_specs=pl.BlockSpec((half, part), lambda i: (0, i)),
        out_shape=jax.ShapeDtypeStruct((half, nz * part), BF),
        compiler_params=pltpu.CompilerParams(vmem_limit_bytes=VMEM_BYTES),
        cost_estimate=pl.CostEstimate(flops=4 * 10**9, bytes_accessed=8 * half * part, transcendentals=0),
    )(ours, gathered)


def head_kernel(weight_ref, head_ref, out_ref):
    rows = weight_ref.shape[0]
    for index in range(out_ref.shape[0]):
        out_ref[index, :rows, :] = weight_ref[...]
        out_ref[index, rows:, :] = head_ref[...]


def with_head(proj_weight, cotangent, nz):
    rows, cols = proj_weight.shape
    return pl.pallas_call(
        head_kernel,
        grid=(1,),
        in_specs=[
            pl.BlockSpec((rows, cols), lambda i: (0, 0)),
            pl.BlockSpec((16, cols), lambda i: (0, 0)),
        ],
        out_specs=pl.BlockSpec((nz, rows + 16, cols), lambda i: (0, 0, 0)),
        out_shape=jax.ShapeDtypeStruct((nz, rows + 16, cols), BF),
        compiler_params=pltpu.CompilerParams(vmem_limit_bytes=60 * 1024 * 1024),
    )(proj_weight, cotangent)


def spread(value, axes):
    return exchange(jnp.broadcast_to(value[None], (lax.axis_size(axes),) + value.shape), axes)


def swap(value):
    return lax.ppermute(value, C, [(0, 1), (1, 0)])


def body(tokens, proj_weight, cotangent, filters):
    nz = lax.axis_size(ZH)
    nxy = lax.axis_size((X, Y))
    nzl = lax.axis_size(ZL)
    ndp = nz * nxy
    rows, cols = proj_weight.shape
    own_tokens, depth = tokens.shape

    slab_len = cotangent.shape[0]
    core, chip = lax.axis_index(C), lax.axis_index(ZL)
    direct = [tokens] + [None] * (nzl - 1)
    for steps in (2, 1, 3):
        direct[steps] = from_ahead(tokens, ZL, steps)

    zh, xy = lax.axis_index(ZH), lax.axis_index((X, Y))
    column = exchange(with_head(proj_weight, cotangent, nz), ZH)
    head = lax.dynamic_index_in_dim(column, zh, 0, keepdims=False)[rows : rows + 8]
    ahead = lax.dynamic_index_in_dim(column, (zh + 1) % nz, 0, keepdims=False)[rows : rows + 8]
    column = column[:, :rows].reshape(nz * rows, cols)
    gathered = spread(jnp.concatenate([column, head, ahead], 0), (X, Y))
    heads = lax.dynamic_index_in_dim(gathered, (xy + 1) % nxy, 0, keepdims=False)[nz * rows :]
    following = jnp.where(xy == nxy - 1, heads[8:], heads[:8])
    following = jnp.where(zh * nxy + xy == ndp - 1, jnp.zeros((), BF), following).astype(F32)
    chunks = direct + [swap(value) for value in direct]
    slab = in_order(chunks)
    packed, for_other, ours = local_products(
        core, slab, gathered, cotangent, following, filters, nz, rows
    )
    total = jnp.sum(exchange(packed, (X, Y)).astype(F32), axis=0)

    here = own_products(ours, gathered, nz, rows)
    chip_sum = (here.astype(F32) + swap(for_other).astype(F32)).astype(BF)
    chip_sum = chip_sum.reshape(nzl, own_tokens, depth)
    summed = lax.dynamic_index_in_dim(chip_sum, chip, 0, keepdims=False).astype(F32)
    for steps in (2, 1, 3):
        outgoing = lax.dynamic_index_in_dim(chip_sum, (chip - steps) % nzl, 0, keepdims=False)
        summed = summed + from_ahead(outgoing, ZL, steps).astype(F32)
    input_grad = summed.astype(BF)

    blocks = total[: nz * rows].astype(BF).reshape(nz, rows, cols)
    tail = split_rows(joined_rows(total[nz * rows :]))
    packed = jnp.concatenate([blocks, jnp.broadcast_to(tail[None], (nz, 16, cols))], 1)
    arrived = exchange(packed, ZH)
    arrived, input_grad = lax.optimization_barrier((arrived, input_grad))
    total = jnp.sum(arrived.astype(F32), axis=0)
    weight_grad = total[:rows].astype(BF)
    filter_grad = joined_rows(total[rows:])[:TAPS]
    return input_grad, weight_grad, filter_grad


def solution(mesh):
    fine = Mesh(mesh.devices.reshape(4, 4, 4, 4, 2), (ZH, X, Y, ZL, C))
    dp, seq = (ZH, X, Y), (ZL, C)
    in_specs = (P(dp + seq, None), P(dp, seq), P(dp, seq), P(None, seq))
    out_specs = (P(dp + seq, None), P(dp, seq), P(None, seq))
    return jax.shard_map(body, mesh=fine, in_specs=in_specs, out_specs=out_specs, check_vma=False)
```

```python
import jax
import jax.numpy as jnp
from jax import lax
from jax.experimental import pallas as pl
from jax.experimental.pallas import tpu as pltpu
from jax.sharding import Mesh, PartitionSpec as P

TAPS = 7
VMEM_BYTES = 12 * 1024 * 1024
PRODUCTS_VMEM = 49 * 1024 * 1024
BF = jnp.bfloat16
F32 = jnp.float32
ZH, X, Y, ZL, C = "zh", "x", "y", "zl", "c"


def split_rows(value):
    high = value.astype(BF)
    return jnp.concatenate([high, (value - high.astype(F32)).astype(BF)], 0)


def joined_rows(value):
    half = value.shape[0] // 2
    return value[:half] + value[half:]


def exchange(value, axes):
    return lax.all_to_all(value, axes, split_axis=0, concat_axis=0, tiled=True)


def from_ahead(value, axis, steps):
    count = lax.axis_size(axis)
    return lax.ppermute(value, axis, [(source, (source - steps) % count) for source in range(count)])


def order_kernel(*refs):
    chunks, (slab_ref, done) = refs[:-2], refs[-2:]
    count, chips = chunks[0].shape[0], len(chunks) // 2
    core, chip = lax.axis_index(C), lax.axis_index(ZL)
    copies = []
    for index, chunk in enumerate(chunks):
        source = lax.rem(chip + index % chips, chips)
        place = 2 * source + (core if index < chips else 1 - core)
        rows = pl.ds(pl.multiple_of(place * count, count), count)
        copies.append(pltpu.make_async_copy(chunk, slab_ref.at[rows, :], done.at[index]))
        copies[-1].start()
    for copy in copies:
        copy.wait()


def in_order(chunks):
    count, depth = chunks[0].shape
    return pl.pallas_call(
        order_kernel,
        in_specs=[pl.BlockSpec(memory_space=pl.ANY) for _ in chunks],
        out_specs=pl.BlockSpec(memory_space=pltpu.HBM),
        out_shape=pltpu.HBM((len(chunks) * count, depth), BF),
        scratch_shapes=[pltpu.SemaphoreType.DMA((len(chunks),))],
        compiler_params=pltpu.CompilerParams(vmem_limit_bytes=VMEM_BYTES),
        cost_estimate=pl.CostEstimate(
            flops=8 * 10**9, bytes_accessed=4 * len(chunks) * count * depth, transcendentals=0
        ),
    )(*chunks)


def products_kernel(
    core_ref, slab_ref, weight_ref, cotangent_ref, following_ref, filters_ref,
    packed_ref, theirs_out, ours_out, extended_ref, grad_ref, theirs_ref, featured_ref,
):
    step, core = pl.program_id(0), core_ref[0]
    slab_len, cols = grad_ref.shape
    nxy, rows, _ = weight_ref.shape
    half = theirs_ref.shape[0]
    own = slab_len // 8

    @pl.when(step == 0)
    def _():
        extended_ref[:slab_len, :] = cotangent_ref[...].astype(F32)
        extended_ref[slab_len:, :] = following_ref[...]
        grad_feat = filters_ref[0:1, :] * extended_ref[0:slab_len, :]
        for tap in range(1, TAPS):
            grad_feat = grad_feat + filters_ref[tap : tap + 1, :] * extended_ref[tap : tap + slab_len, :]
        grad_ref[...] = grad_feat.astype(BF)
        for index in range(half // own):
            there = pl.ds(pl.multiple_of((2 * index + 1 - core) * own, own), own)
            here = pl.ds(pl.multiple_of((2 * index + core) * own, own), own)
            theirs_ref[index * own : (index + 1) * own, :] = grad_ref[there, :]
            ours_out[index * own : (index + 1) * own, :] = grad_ref[here, :]

    weight = weight_ref[...].reshape(nxy * rows, cols)
    contract_cols = (((1,), (1,)), ((), ()))
    theirs_out[...] = lax.dot_general(
        theirs_ref[...], weight, contract_cols, preferred_element_type=F32
    ).astype(BF)
    products = lax.dot_general(
        slab_ref[...], grad_ref[...], (((0,), (0,)), ((), ())), preferred_element_type=F32
    )
    place = pl.ds(pl.multiple_of(step * rows, rows), rows)
    packed_ref[:, place, :] = products.astype(BF).reshape(nxy, rows, cols)
    term = jnp.dot(slab_ref[...], weight, preferred_element_type=F32)

    @pl.when(step == 0)
    def _():
        featured_ref[...] = term

    @pl.when(step > 0)
    def _():
        featured_ref[...] += term

    @pl.when(step == pl.num_programs(0) - 1)
    def _():
        featured = featured_ref[...].astype(BF).astype(F32)
        sums = [
            jnp.sum(featured * extended_ref[tap : tap + slab_len, :], axis=0, keepdims=True)
            for tap in range(TAPS)
        ]
        tail = split_rows(jnp.concatenate(sums + [jnp.zeros((1, cols), F32)], 0))
        packed_ref[:, pl.num_programs(0) * rows :, :] = jnp.broadcast_to(tail[None], (nxy, 16, cols))


def local_products(core, slab, gathered, cotangent, following, filters, nz, rows):
    slab_len, depth = slab.shape
    nxy, _, cols = gathered.shape
    part = nxy * rows
    half = slab_len // 2
    return pl.pallas_call(
        products_kernel,
        grid_spec=pltpu.PrefetchScalarGridSpec(
            num_scalar_prefetch=1,
            grid=(nz,),
            in_specs=[
                pl.BlockSpec((slab_len, part), lambda i, _: (0, i)),
                pl.BlockSpec((nxy, rows, cols), lambda i, _: (0, i, 0)),
                pl.BlockSpec((slab_len, cols), lambda i, _: (0, 0)),
                pl.BlockSpec(following.shape, lambda i, _: (0, 0)),
                pl.BlockSpec(filters.shape, lambda i, _: (0, 0)),
            ],
            out_specs=[
                pl.BlockSpec((nxy, nz * rows + 16, cols), lambda i, _: (0, 0, 0)),
                pl.BlockSpec((half, part), lambda i, _: (0, i)),
                pl.BlockSpec((half, cols), lambda i, _: (0, 0)),
            ],
            scratch_shapes=[
                pltpu.VMEM((slab_len + 8, cols), F32),
                pltpu.VMEM((slab_len, cols), BF),
                pltpu.VMEM((half, cols), BF),
                pltpu.VMEM((slab_len, cols), F32),
            ],
        ),
        out_shape=[
            jax.ShapeDtypeStruct((nxy, nz * rows + 16, cols), BF),
            jax.ShapeDtypeStruct((half, depth), BF),
            jax.ShapeDtypeStruct((half, cols), BF),
        ],
        compiler_params=pltpu.CompilerParams(vmem_limit_bytes=PRODUCTS_VMEM),
        cost_estimate=pl.CostEstimate(
            flops=6 * slab_len * depth * cols, bytes_accessed=6 * slab_len * depth, transcendentals=0
        ),
    )(core.reshape(1).astype(jnp.int32), slab, gathered, cotangent, following, filters)


def chip_sum_kernel(ours_ref, weight_ref, other_ref, *refs):
    outs, sum_ref = refs[:-1], refs[-1]
    weight = weight_ref[...].reshape(-1, ours_ref.shape[1])
    here = lax.dot_general(
        ours_ref[...], weight, (((1,), (1,)), ((), ())), preferred_element_type=F32
    )
    sum_ref[...] = (here + other_ref[...].astype(F32)).astype(BF)
    chips, chip = len(outs), lax.axis_index(ZL)
    count = outs[0].shape[0]
    for steps, out_ref in enumerate(outs):
        target = lax.rem(chip + chips - steps, chips)
        out_ref[...] = sum_ref[pl.ds(pl.multiple_of(target * count, count), count), :]


def chip_sums(ours, gathered, from_other, nz, rows, chips):
    half, cols = ours.shape
    nxy = gathered.shape[0]
    part = nxy * rows
    return pl.pallas_call(
        chip_sum_kernel,
        grid=(nz,),
        in_specs=[
            pl.BlockSpec((half, cols), lambda i: (0, 0)),
            pl.BlockSpec((nxy, rows, cols), lambda i: (0, i, 0)),
            pl.BlockSpec((half, part), lambda i: (0, i)),
        ],
        out_specs=[pl.BlockSpec((half // chips, part), lambda i: (0, i)) for _ in range(chips)],
        out_shape=[jax.ShapeDtypeStruct((half // chips, nz * part), BF) for _ in range(chips)],
        scratch_shapes=[pltpu.VMEM((half, part), BF)],
        compiler_params=pltpu.CompilerParams(vmem_limit_bytes=VMEM_BYTES),
        cost_estimate=pl.CostEstimate(
            flops=2 * half * cols * nz * part, bytes_accessed=8 * half * nz * part, transcendentals=0
        ),
    )(ours, gathered, from_other)


def head_kernel(weight_ref, head_ref, out_ref):
    rows = weight_ref.shape[0]
    for index in range(out_ref.shape[0]):
        out_ref[index, :rows, :] = weight_ref[...]
        out_ref[index, rows:, :] = head_ref[...]


def with_head(proj_weight, cotangent, nz):
    rows, cols = proj_weight.shape
    return pl.pallas_call(
        head_kernel,
        grid=(1,),
        in_specs=[
            pl.BlockSpec((rows, cols), lambda i: (0, 0)),
            pl.BlockSpec((16, cols), lambda i: (0, 0)),
        ],
        out_specs=pl.BlockSpec((nz, rows + 16, cols), lambda i: (0, 0, 0)),
        out_shape=jax.ShapeDtypeStruct((nz, rows + 16, cols), BF),
        compiler_params=pltpu.CompilerParams(vmem_limit_bytes=60 * 1024 * 1024),
    )(proj_weight, cotangent)


def spread(value, axes):
    return exchange(jnp.broadcast_to(value[None], (lax.axis_size(axes),) + value.shape), axes)


def swap(value):
    return lax.ppermute(value, C, [(0, 1), (1, 0)])


def body(tokens, proj_weight, cotangent, filters):
    nz = lax.axis_size(ZH)
    nxy = lax.axis_size((X, Y))
    nzl = lax.axis_size(ZL)
    ndp = nz * nxy
    rows, cols = proj_weight.shape
    own_tokens, depth = tokens.shape

    slab_len = cotangent.shape[0]
    core, chip = lax.axis_index(C), lax.axis_index(ZL)
    direct = [tokens] + [None] * (nzl - 1)
    for steps in (2, 1, 3):
        direct[steps] = from_ahead(tokens, ZL, steps)

    zh, xy = lax.axis_index(ZH), lax.axis_index((X, Y))
    column = exchange(with_head(proj_weight, cotangent, nz), ZH)
    head = lax.dynamic_index_in_dim(column, zh, 0, keepdims=False)[rows : rows + 8]
    ahead = lax.dynamic_index_in_dim(column, (zh + 1) % nz, 0, keepdims=False)[rows : rows + 8]
    column = column[:, :rows].reshape(nz * rows, cols)
    gathered = spread(jnp.concatenate([column, head, ahead], 0), (X, Y))
    heads = lax.dynamic_index_in_dim(gathered, (xy + 1) % nxy, 0, keepdims=False)[nz * rows :]
    following = jnp.where(xy == nxy - 1, heads[8:], heads[:8])
    following = jnp.where(zh * nxy + xy == ndp - 1, jnp.zeros((), BF), following).astype(F32)
    chunks = direct + [swap(value) for value in direct]
    slab = in_order(chunks)
    packed, for_other, ours = local_products(
        core, slab, gathered, cotangent, following, filters, nz, rows
    )
    total = jnp.sum(exchange(packed, (X, Y)).astype(F32), axis=0)

    pieces = chip_sums(ours, gathered, swap(for_other), nz, rows, nzl)
    summed = pieces[0].astype(F32)
    for steps in (2, 1, 3):
        summed = summed + from_ahead(pieces[steps], ZL, steps).astype(F32)
    input_grad = summed.astype(BF)

    blocks = total[: nz * rows].astype(BF).reshape(nz, rows, cols)
    tail = split_rows(joined_rows(total[nz * rows :]))
    packed = jnp.concatenate([blocks, jnp.broadcast_to(tail[None], (nz, 16, cols))], 1)
    arrived = exchange(packed, ZH)
    arrived, input_grad = lax.optimization_barrier((arrived, input_grad))
    total = jnp.sum(arrived.astype(F32), axis=0)
    weight_grad = total[:rows].astype(BF)
    filter_grad = joined_rows(total[rows:])[:TAPS]
    return input_grad, weight_grad, filter_grad


def solution(mesh):
    fine = Mesh(mesh.devices.reshape(4, 4, 4, 4, 2), (ZH, X, Y, ZL, C))
    dp, seq = (ZH, X, Y), (ZL, C)
    in_specs = (P(dp + seq, None), P(dp, seq), P(dp, seq), P(None, seq))
    out_specs = (P(dp + seq, None), P(dp, seq), P(None, seq))
    return jax.shard_map(body, mesh=fine, in_specs=in_specs, out_specs=out_specs, check_vma=False)
```

```python
import jax
import jax.numpy as jnp
from jax import lax
from jax.experimental import pallas as pl
from jax.experimental.pallas import tpu as pltpu
from jax.sharding import Mesh, PartitionSpec as P

TAPS = 7
ORDER = (0, 2, 1, 3)
VMEM_BYTES = 12 * 1024 * 1024
PRODUCTS_VMEM = 49 * 1024 * 1024
BF = jnp.bfloat16
F32 = jnp.float32
ZH, X, Y, ZL, C = "zh", "x", "y", "zl", "c"


def split_rows(value):
    high = value.astype(BF)
    return jnp.concatenate([high, (value - high.astype(F32)).astype(BF)], 0)


def joined_rows(value):
    half = value.shape[0] // 2
    return value[:half] + value[half:]


def exchange(value, axes):
    return lax.all_to_all(value, axes, split_axis=0, concat_axis=0, tiled=True)


def from_ahead(value, axis, steps):
    count = lax.axis_size(axis)
    return lax.ppermute(value, axis, [(source, (source - steps) % count) for source in range(count)])


def order_kernel(*refs):
    chunks, (slab_ref, done) = refs[:-2], refs[-2:]
    count, chips = chunks[0].shape[0], len(chunks) // 2
    core, chip = lax.axis_index(C), lax.axis_index(ZL)
    copies = []
    for index, chunk in enumerate(chunks):
        source = lax.rem(chip + ORDER[index % chips], chips)
        place = 2 * source + (core if index < chips else 1 - core)
        rows = pl.ds(pl.multiple_of(place * count, count), count)
        copies.append(pltpu.make_async_copy(chunk, slab_ref.at[rows, :], done.at[index]))
        copies[-1].start()
    for copy in copies:
        copy.wait()


def in_order(chunks):
    count, depth = chunks[0].shape
    return pl.pallas_call(
        order_kernel,
        in_specs=[pl.BlockSpec(memory_space=pl.ANY) for _ in chunks],
        out_specs=pl.BlockSpec(memory_space=pltpu.HBM),
        out_shape=pltpu.HBM((len(chunks) * count, depth), BF),
        scratch_shapes=[pltpu.SemaphoreType.DMA((len(chunks),))],
        compiler_params=pltpu.CompilerParams(vmem_limit_bytes=VMEM_BYTES),
        cost_estimate=pl.CostEstimate(
            flops=8 * 10**9, bytes_accessed=4 * len(chunks) * count * depth, transcendentals=0
        ),
    )(*chunks)


def products_kernel(
    core_ref, slab_ref, weight_ref, cotangent_ref, following_ref, filters_ref,
    packed_ref, theirs_out, ours_out, extended_ref, grad_ref, theirs_ref, featured_ref,
):
    step, core = pl.program_id(0), core_ref[0]
    slab_len, cols = grad_ref.shape
    nxy, rows, _ = weight_ref.shape
    half = theirs_ref.shape[0]
    own = slab_len // 8

    @pl.when(step == 0)
    def _():
        extended_ref[:slab_len, :] = cotangent_ref[...].astype(F32)
        extended_ref[slab_len:, :] = following_ref[...]
        grad_feat = filters_ref[0:1, :] * extended_ref[0:slab_len, :]
        for tap in range(1, TAPS):
            grad_feat = grad_feat + filters_ref[tap : tap + 1, :] * extended_ref[tap : tap + slab_len, :]
        grad_ref[...] = grad_feat.astype(BF)
        for index in range(half // own):
            there = pl.ds(pl.multiple_of((2 * index + 1 - core) * own, own), own)
            here = pl.ds(pl.multiple_of((2 * index + core) * own, own), own)
            theirs_ref[index * own : (index + 1) * own, :] = grad_ref[there, :]
            ours_out[index * own : (index + 1) * own, :] = grad_ref[here, :]

    weight = weight_ref[...].reshape(nxy * rows, cols)
    contract_cols = (((1,), (1,)), ((), ()))
    theirs_out[...] = lax.dot_general(
        theirs_ref[...], weight, contract_cols, preferred_element_type=F32
    ).astype(BF)
    products = lax.dot_general(
        slab_ref[...], grad_ref[...], (((0,), (0,)), ((), ())), preferred_element_type=F32
    )
    place = pl.ds(pl.multiple_of(step * rows, rows), rows)
    packed_ref[:, place, :] = products.astype(BF).reshape(nxy, rows, cols)
    term = jnp.dot(slab_ref[...], weight, preferred_element_type=F32)

    @pl.when(step == 0)
    def _():
        featured_ref[...] = term

    @pl.when(step > 0)
    def _():
        featured_ref[...] += term

    @pl.when(step == pl.num_programs(0) - 1)
    def _():
        featured = featured_ref[...].astype(BF).astype(F32)
        sums = [
            jnp.sum(featured * extended_ref[tap : tap + slab_len, :], axis=0, keepdims=True)
            for tap in range(TAPS)
        ]
        tail = split_rows(jnp.concatenate(sums + [jnp.zeros((1, cols), F32)], 0))
        packed_ref[:, pl.num_programs(0) * rows :, :] = jnp.broadcast_to(tail[None], (nxy, 16, cols))


def local_products(core, slab, gathered, cotangent, following, filters, nz, rows):
    slab_len, depth = slab.shape
    nxy, _, cols = gathered.shape
    part = nxy * rows
    half = slab_len // 2
    return pl.pallas_call(
        products_kernel,
        grid_spec=pltpu.PrefetchScalarGridSpec(
            num_scalar_prefetch=1,
            grid=(nz,),
            in_specs=[
                pl.BlockSpec((slab_len, part), lambda i, _: (0, i)),
                pl.BlockSpec((nxy, rows, cols), lambda i, _: (0, i, 0)),
                pl.BlockSpec((slab_len, cols), lambda i, _: (0, 0)),
                pl.BlockSpec(following.shape, lambda i, _: (0, 0)),
                pl.BlockSpec(filters.shape, lambda i, _: (0, 0)),
            ],
            out_specs=[
                pl.BlockSpec((nxy, nz * rows + 16, cols), lambda i, _: (0, 0, 0)),
                pl.BlockSpec((half, part), lambda i, _: (0, i)),
                pl.BlockSpec((half, cols), lambda i, _: (0, 0)),
            ],
            scratch_shapes=[
                pltpu.VMEM((slab_len + 8, cols), F32),
                pltpu.VMEM((slab_len, cols), BF),
                pltpu.VMEM((half, cols), BF),
                pltpu.VMEM((slab_len, cols), F32),
            ],
        ),
        out_shape=[
            jax.ShapeDtypeStruct((nxy, nz * rows + 16, cols), BF),
            jax.ShapeDtypeStruct((half, depth), BF),
            jax.ShapeDtypeStruct((half, cols), BF),
        ],
        compiler_params=pltpu.CompilerParams(vmem_limit_bytes=PRODUCTS_VMEM),
        cost_estimate=pl.CostEstimate(
            flops=6 * slab_len * depth * cols, bytes_accessed=6 * slab_len * depth, transcendentals=0
        ),
    )(core.reshape(1).astype(jnp.int32), slab, gathered, cotangent, following, filters)


def chip_sum_kernel(ours_ref, weight_ref, other_ref, *refs):
    outs, sum_ref = refs[:-1], refs[-1]
    weight = weight_ref[...].reshape(-1, ours_ref.shape[1])
    here = lax.dot_general(
        ours_ref[...], weight, (((1,), (1,)), ((), ())), preferred_element_type=F32
    )
    sum_ref[...] = (here + other_ref[...].astype(F32)).astype(BF)
    chips, chip = len(outs), lax.axis_index(ZL)
    count = outs[0].shape[0]
    for steps, out_ref in enumerate(outs):
        target = lax.rem(chip + chips - steps, chips)
        out_ref[...] = sum_ref[pl.ds(pl.multiple_of(target * count, count), count), :]


def chip_sums(ours, gathered, from_other, nz, rows, chips):
    half, cols = ours.shape
    nxy = gathered.shape[0]
    part = nxy * rows
    return pl.pallas_call(
        chip_sum_kernel,
        grid=(nz,),
        in_specs=[
            pl.BlockSpec((half, cols), lambda i: (0, 0)),
            pl.BlockSpec((nxy, rows, cols), lambda i: (0, i, 0)),
            pl.BlockSpec((half, part), lambda i: (0, i)),
        ],
        out_specs=[pl.BlockSpec((half // chips, part), lambda i: (0, i)) for _ in range(chips)],
        out_shape=[jax.ShapeDtypeStruct((half // chips, nz * part), BF) for _ in range(chips)],
        scratch_shapes=[pltpu.VMEM((half, part), BF)],
        compiler_params=pltpu.CompilerParams(vmem_limit_bytes=VMEM_BYTES),
        cost_estimate=pl.CostEstimate(
            flops=2 * half * cols * nz * part, bytes_accessed=8 * half * nz * part, transcendentals=0
        ),
    )(ours, gathered, from_other)


def head_kernel(weight_ref, head_ref, out_ref):
    rows = weight_ref.shape[0]
    for index in range(out_ref.shape[0]):
        out_ref[index, :rows, :] = weight_ref[...]
        out_ref[index, rows:, :] = head_ref[...]


def with_head(proj_weight, cotangent, nz):
    rows, cols = proj_weight.shape
    return pl.pallas_call(
        head_kernel,
        grid=(1,),
        in_specs=[
            pl.BlockSpec((rows, cols), lambda i: (0, 0)),
            pl.BlockSpec((16, cols), lambda i: (0, 0)),
        ],
        out_specs=pl.BlockSpec((nz, rows + 16, cols), lambda i: (0, 0, 0)),
        out_shape=jax.ShapeDtypeStruct((nz, rows + 16, cols), BF),
        compiler_params=pltpu.CompilerParams(vmem_limit_bytes=60 * 1024 * 1024),
    )(proj_weight, cotangent)


def spread(value, axes):
    return exchange(jnp.broadcast_to(value[None], (lax.axis_size(axes),) + value.shape), axes)


def swap(value):
    return lax.ppermute(value, C, [(0, 1), (1, 0)])


def body(tokens, proj_weight, cotangent, filters):
    nz = lax.axis_size(ZH)
    nxy = lax.axis_size((X, Y))
    nzl = lax.axis_size(ZL)
    ndp = nz * nxy
    rows, cols = proj_weight.shape
    own_tokens, depth = tokens.shape

    slab_len = cotangent.shape[0]
    core, chip = lax.axis_index(C), lax.axis_index(ZL)
    direct = [tokens] + [None] * (nzl - 1)
    for steps in (2, 1, 3):
        direct[steps] = from_ahead(tokens, ZL, steps)

    zh, xy = lax.axis_index(ZH), lax.axis_index((X, Y))
    column = exchange(with_head(proj_weight, cotangent, nz), ZH)
    head = lax.dynamic_index_in_dim(column, zh, 0, keepdims=False)[rows : rows + 8]
    ahead = lax.dynamic_index_in_dim(column, (zh + 1) % nz, 0, keepdims=False)[rows : rows + 8]
    column = column[:, :rows].reshape(nz * rows, cols)
    gathered = spread(jnp.concatenate([column, head, ahead], 0), (X, Y))
    heads = lax.dynamic_index_in_dim(gathered, (xy + 1) % nxy, 0, keepdims=False)[nz * rows :]
    following = jnp.where(xy == nxy - 1, heads[8:], heads[:8])
    following = jnp.where(zh * nxy + xy == ndp - 1, jnp.zeros((), BF), following).astype(F32)
    direct = [direct[steps] for steps in ORDER]
    chunks = direct + [swap(value) for value in direct]
    slab = in_order(chunks)
    packed, for_other, ours = local_products(
        core, slab, gathered, cotangent, following, filters, nz, rows
    )
    total = jnp.sum(exchange(packed, (X, Y)).astype(F32), axis=0)

    pieces = chip_sums(ours, gathered, swap(for_other), nz, rows, nzl)
    summed = pieces[0].astype(F32)
    for steps in (2, 1, 3):
        summed = summed + from_ahead(pieces[steps], ZL, steps).astype(F32)
    input_grad = summed.astype(BF)

    blocks = total[: nz * rows].astype(BF).reshape(nz, rows, cols)
    tail = split_rows(joined_rows(total[nz * rows :]))
    packed = jnp.concatenate([blocks, jnp.broadcast_to(tail[None], (nz, 16, cols))], 1)
    arrived = exchange(packed, ZH)
    arrived, input_grad = lax.optimization_barrier((arrived, input_grad))
    total = jnp.sum(arrived.astype(F32), axis=0)
    weight_grad = total[:rows].astype(BF)
    filter_grad = joined_rows(total[rows:])[:TAPS]
    return input_grad, weight_grad, filter_grad


def solution(mesh):
    fine = Mesh(mesh.devices.reshape(4, 4, 4, 4, 2), (ZH, X, Y, ZL, C))
    dp, seq = (ZH, X, Y), (ZL, C)
    in_specs = (P(dp + seq, None), P(dp, seq), P(dp, seq), P(None, seq))
    out_specs = (P(dp + seq, None), P(dp, seq), P(None, seq))
    return jax.shard_map(body, mesh=fine, in_specs=in_specs, out_specs=out_specs, check_vma=False)
```

```python
import jax
import jax.numpy as jnp
from jax import lax
from jax.experimental import pallas as pl
from jax.experimental.pallas import tpu as pltpu
from jax.sharding import Mesh, PartitionSpec as P

TAPS = 7
ORDER = (0, 2, 1, 3)
VMEM_BYTES = 12 * 1024 * 1024
PRODUCTS_VMEM = 49 * 1024 * 1024
BF = jnp.bfloat16
F32 = jnp.float32
ZH, X, Y, ZL, C = "zh", "x", "y", "zl", "c"


def split_rows(value):
    high = value.astype(BF)
    return jnp.concatenate([high, (value - high.astype(F32)).astype(BF)], 0)


def joined_rows(value):
    half = value.shape[0] // 2
    return value[:half] + value[half:]


def exchange(value, axes):
    return lax.all_to_all(value, axes, split_axis=0, concat_axis=0, tiled=True)


def from_ahead(value, axis, steps):
    count = lax.axis_size(axis)
    return lax.ppermute(value, axis, [(source, (source - steps) % count) for source in range(count)])


def order_kernel(*refs):
    chunks, (slab_ref, done) = refs[:-2], refs[-2:]
    count, chips = chunks[0].shape[0], len(chunks) // 2
    core, chip = lax.axis_index(C), lax.axis_index(ZL)
    copies = []
    for index, chunk in enumerate(chunks):
        source = lax.rem(chip + ORDER[index % chips], chips)
        place = 2 * source + (core if index < chips else 1 - core)
        rows = pl.ds(pl.multiple_of(place * count, count), count)
        copies.append(pltpu.make_async_copy(chunk, slab_ref.at[rows, :], done.at[index]))
        copies[-1].start()
    for copy in copies:
        copy.wait()


def in_order(chunks):
    count, depth = chunks[0].shape
    return pl.pallas_call(
        order_kernel,
        in_specs=[pl.BlockSpec(memory_space=pl.ANY) for _ in chunks],
        out_specs=pl.BlockSpec(memory_space=pltpu.HBM),
        out_shape=pltpu.HBM((len(chunks) * count, depth), BF),
        scratch_shapes=[pltpu.SemaphoreType.DMA((len(chunks),))],
        compiler_params=pltpu.CompilerParams(vmem_limit_bytes=VMEM_BYTES),
        cost_estimate=pl.CostEstimate(
            flops=6 * 10**9, bytes_accessed=4 * len(chunks) * count * depth, transcendentals=0
        ),
    )(*chunks)


def products_kernel(
    core_ref, slab_ref, weight_ref, cotangent_ref, following_ref, filters_ref,
    packed_ref, theirs_out, ours_out, extended_ref, grad_ref, theirs_ref, featured_ref,
):
    step, core = pl.program_id(0), core_ref[0]
    slab_len, cols = grad_ref.shape
    nxy, rows, _ = weight_ref.shape
    half = theirs_ref.shape[0]
    own = slab_len // 8

    @pl.when(step == 0)
    def _():
        extended_ref[:slab_len, :] = cotangent_ref[...].astype(F32)
        extended_ref[slab_len:, :] = following_ref[...]
        grad_feat = filters_ref[0:1, :] * extended_ref[0:slab_len, :]
        for tap in range(1, TAPS):
            grad_feat = grad_feat + filters_ref[tap : tap + 1, :] * extended_ref[tap : tap + slab_len, :]
        grad_ref[...] = grad_feat.astype(BF)
        for index in range(half // own):
            there = pl.ds(pl.multiple_of((2 * index + 1 - core) * own, own), own)
            here = pl.ds(pl.multiple_of((2 * index + core) * own, own), own)
            theirs_ref[index * own : (index + 1) * own, :] = grad_ref[there, :]
            ours_out[index * own : (index + 1) * own, :] = grad_ref[here, :]

    weight = weight_ref[...].reshape(nxy * rows, cols)
    contract_cols = (((1,), (1,)), ((), ()))
    theirs_out[...] = lax.dot_general(
        theirs_ref[...], weight, contract_cols, preferred_element_type=F32
    ).astype(BF)
    products = lax.dot_general(
        slab_ref[...], grad_ref[...], (((0,), (0,)), ((), ())), preferred_element_type=F32
    )
    place = pl.ds(pl.multiple_of(step * rows, rows), rows)
    packed_ref[:, place, :] = products.astype(BF).reshape(nxy, rows, cols)
    term = jnp.dot(slab_ref[...], weight, preferred_element_type=F32)

    @pl.when(step == 0)
    def _():
        featured_ref[...] = term

    @pl.when(step > 0)
    def _():
        featured_ref[...] += term

    @pl.when(step == pl.num_programs(0) - 1)
    def _():
        featured = featured_ref[...].astype(BF).astype(F32)
        sums = [
            jnp.sum(featured * extended_ref[tap : tap + slab_len, :], axis=0, keepdims=True)
            for tap in range(TAPS)
        ]
        tail = split_rows(jnp.concatenate(sums + [jnp.zeros((1, cols), F32)], 0))
        packed_ref[:, pl.num_programs(0) * rows :, :] = jnp.broadcast_to(tail[None], (nxy, 16, cols))


def local_products(core, slab, gathered, cotangent, following, filters, nz, rows):
    slab_len, depth = slab.shape
    nxy, _, cols = gathered.shape
    part = nxy * rows
    half = slab_len // 2
    return pl.pallas_call(
        products_kernel,
        grid_spec=pltpu.PrefetchScalarGridSpec(
            num_scalar_prefetch=1,
            grid=(nz,),
            in_specs=[
                pl.BlockSpec((slab_len, part), lambda i, _: (0, i)),
                pl.BlockSpec((nxy, rows, cols), lambda i, _: (0, i, 0)),
                pl.BlockSpec((slab_len, cols), lambda i, _: (0, 0)),
                pl.BlockSpec(following.shape, lambda i, _: (0, 0)),
                pl.BlockSpec(filters.shape, lambda i, _: (0, 0)),
            ],
            out_specs=[
                pl.BlockSpec((nxy, nz * rows + 16, cols), lambda i, _: (0, 0, 0)),
                pl.BlockSpec((half, part), lambda i, _: (0, i)),
                pl.BlockSpec((half, cols), lambda i, _: (0, 0)),
            ],
            scratch_shapes=[
                pltpu.VMEM((slab_len + 8, cols), F32),
                pltpu.VMEM((slab_len, cols), BF),
                pltpu.VMEM((half, cols), BF),
                pltpu.VMEM((slab_len, cols), F32),
            ],
        ),
        out_shape=[
            jax.ShapeDtypeStruct((nxy, nz * rows + 16, cols), BF),
            jax.ShapeDtypeStruct((half, depth), BF),
            jax.ShapeDtypeStruct((half, cols), BF),
        ],
        compiler_params=pltpu.CompilerParams(vmem_limit_bytes=PRODUCTS_VMEM),
        cost_estimate=pl.CostEstimate(
            flops=6 * slab_len * depth * cols, bytes_accessed=6 * slab_len * depth, transcendentals=0
        ),
    )(core.reshape(1).astype(jnp.int32), slab, gathered, cotangent, following, filters)


def chip_sum_kernel(ours_ref, weight_ref, other_ref, *refs):
    outs, sum_ref = refs[:-1], refs[-1]
    weight = weight_ref[...].reshape(-1, ours_ref.shape[1])
    here = lax.dot_general(
        ours_ref[...], weight, (((1,), (1,)), ((), ())), preferred_element_type=F32
    )
    sum_ref[...] = (here + other_ref[...].astype(F32)).astype(BF)
    chips, chip = len(outs), lax.axis_index(ZL)
    count = outs[0].shape[0]
    for steps, out_ref in enumerate(outs):
        target = lax.rem(chip + chips - steps, chips)
        out_ref[...] = sum_ref[pl.ds(pl.multiple_of(target * count, count), count), :]


def chip_sums(ours, gathered, from_other, nz, rows, chips):
    half, cols = ours.shape
    nxy = gathered.shape[0]
    part = nxy * rows
    return pl.pallas_call(
        chip_sum_kernel,
        grid=(nz,),
        in_specs=[
            pl.BlockSpec((half, cols), lambda i: (0, 0)),
            pl.BlockSpec((nxy, rows, cols), lambda i: (0, i, 0)),
            pl.BlockSpec((half, part), lambda i: (0, i)),
        ],
        out_specs=[pl.BlockSpec((half // chips, part), lambda i: (0, i)) for _ in range(chips)],
        out_shape=[jax.ShapeDtypeStruct((half // chips, nz * part), BF) for _ in range(chips)],
        scratch_shapes=[pltpu.VMEM((half, part), BF)],
        compiler_params=pltpu.CompilerParams(vmem_limit_bytes=VMEM_BYTES),
        cost_estimate=pl.CostEstimate(
            flops=2 * half * cols * nz * part, bytes_accessed=8 * half * nz * part, transcendentals=0
        ),
    )(ours, gathered, from_other)


def head_kernel(weight_ref, head_ref, out_ref):
    rows = weight_ref.shape[0]
    for index in range(out_ref.shape[0]):
        out_ref[index, :rows, :] = weight_ref[...]
        out_ref[index, rows:, :] = head_ref[...]


def with_head(proj_weight, cotangent, nz):
    rows, cols = proj_weight.shape
    return pl.pallas_call(
        head_kernel,
        grid=(1,),
        in_specs=[
            pl.BlockSpec((rows, cols), lambda i: (0, 0)),
            pl.BlockSpec((16, cols), lambda i: (0, 0)),
        ],
        out_specs=pl.BlockSpec((nz, rows + 16, cols), lambda i: (0, 0, 0)),
        out_shape=jax.ShapeDtypeStruct((nz, rows + 16, cols), BF),
        compiler_params=pltpu.CompilerParams(vmem_limit_bytes=60 * 1024 * 1024),
    )(proj_weight, cotangent)


def spread(value, axes):
    return exchange(jnp.broadcast_to(value[None], (lax.axis_size(axes),) + value.shape), axes)


def swap(value):
    return lax.ppermute(value, C, [(0, 1), (1, 0)])


def body(tokens, proj_weight, cotangent, filters):
    nz = lax.axis_size(ZH)
    nxy = lax.axis_size((X, Y))
    nzl = lax.axis_size(ZL)
    ndp = nz * nxy
    rows, cols = proj_weight.shape
    own_tokens, depth = tokens.shape

    slab_len = cotangent.shape[0]
    core, chip = lax.axis_index(C), lax.axis_index(ZL)
    direct = [tokens] + [None] * (nzl - 1)
    for steps in (2, 1, 3):
        direct[steps] = from_ahead(tokens, ZL, steps)

    zh, xy = lax.axis_index(ZH), lax.axis_index((X, Y))
    column = exchange(with_head(proj_weight, cotangent, nz), ZH)
    head = lax.dynamic_index_in_dim(column, zh, 0, keepdims=False)[rows : rows + 8]
    ahead = lax.dynamic_index_in_dim(column, (zh + 1) % nz, 0, keepdims=False)[rows : rows + 8]
    column = column[:, :rows].reshape(nz * rows, cols)
    gathered = spread(jnp.concatenate([column, head, ahead], 0), (X, Y))
    heads = lax.dynamic_index_in_dim(gathered, (xy + 1) % nxy, 0, keepdims=False)[nz * rows :]
    following = jnp.where(xy == nxy - 1, heads[8:], heads[:8])
    following = jnp.where(zh * nxy + xy == ndp - 1, jnp.zeros((), BF), following).astype(F32)
    direct = [direct[steps] for steps in ORDER]
    chunks = direct + [swap(value) for value in direct]
    slab = in_order(chunks)
    packed, for_other, ours = local_products(
        core, slab, gathered, cotangent, following, filters, nz, rows
    )
    total = jnp.sum(exchange(packed, (X, Y)).astype(F32), axis=0)

    pieces = chip_sums(ours, gathered, swap(for_other), nz, rows, nzl)
    summed = pieces[0].astype(F32)
    for steps in (2, 1, 3):
        summed = summed + from_ahead(pieces[steps], ZL, steps).astype(F32)
    input_grad = summed.astype(BF)

    blocks = total[: nz * rows].astype(BF).reshape(nz, rows, cols)
    tail = split_rows(joined_rows(total[nz * rows :]))
    packed = jnp.concatenate([blocks, jnp.broadcast_to(tail[None], (nz, 16, cols))], 1)
    arrived = exchange(packed, ZH)
    arrived, input_grad = lax.optimization_barrier((arrived, input_grad))
    total = jnp.sum(arrived.astype(F32), axis=0)
    weight_grad = total[:rows].astype(BF)
    filter_grad = joined_rows(total[rows:])[:TAPS]
    return input_grad, weight_grad, filter_grad


def solution(mesh):
    fine = Mesh(mesh.devices.reshape(4, 4, 4, 4, 2), (ZH, X, Y, ZL, C))
    dp, seq = (ZH, X, Y), (ZL, C)
    in_specs = (P(dp + seq, None), P(dp, seq), P(dp, seq), P(None, seq))
    out_specs = (P(dp + seq, None), P(dp, seq), P(None, seq))
    return jax.shard_map(body, mesh=fine, in_specs=in_specs, out_specs=out_specs, check_vma=False)
```
